128 devices in a mesh: sub: 32 (over x, z, core), row: 4 (over y).
Axes of the slice: x: 4, y: 4, z: 4, core: 2. Of those that a mesh axis runs over, the one named last changes fastest.
Arguments:
- forces: float32 [64, 16, 2600], P('sub', None, 'row'), may hold values from -16 to 16
- inverse_h: bfloat16 [64, 2600, 2600], P('sub', 'row'), may hold values from -2 to 12, as said below
- schur_matrix: bfloat16 [64, 2600, 2600], P('sub', 'row'), may hold values from -2 to 12, as said below
- coarse_inv: float32 [1024, 1024], P(('sub', 'row')), may hold values from -1 to 4, as said below
- face_perm: int32 [64, 6, 384], P('sub', None, 'row'), may hold values from 0 to 95, as said below
- corner_rows: int32 [64, 24], P('sub'), may hold values from 576 to 2599, as said below
- corner_ids: int32 [64, 24], P('sub'), may hold values from 0 to 1023
- corner_count: int32 [64], P('sub'), may hold values from 8 to 24, as said below
Outputs:
- multipliers: float32 [64, 16, 2600], P('sub', None, 'row')
- residual: float32 [64, 16, 2600], P('sub', None, 'row')
The draws below stay inside these ranges and needn't reach their ends.
Inputs may be any that keep to these rules, and one draw needn't show every extreme that they name: `inverse_h`: for each subdomain the matrix is symmetric positive definite. `schur_matrix`: for each subdomain the matrix is symmetric positive definite. `coarse_inv`: the matrix is symmetric positive definite. For each subdomain s, face f and block q, entries q * 96 to q * 96 + 95 of face_perm[s, f] are a permutation of 0 to 95, and the same entries of face_perm[partner(s, f), f XOR 1] hold its inverse. `corner_rows`: the 24 rows of a subdomain are distinct and none of them is a face row. `corner_count`: some subdomain has all 24 slots live.
All inputs are finite; a program needn't handle non-finite values.
Results may differ from the reference program's by a relative error of at most 0.009.
The reference program's roundings to bfloat16 on the way (of `spread`) count: a program that leaves them out, or rounds other values in their place, can miss the bound.
Values may be sent and summed in bfloat16 or wider, within the bound.
A program may use at most 128 MiB of HBM per device.

```python
import math
import jax
import jax.numpy as jnp
import numpy as np
from jax import lax

NS = 2600
ROWBLK = 4
BLOCK = 650
FACES = 6
FACEQ = 96
CSLOT = 24
LOADS = 16
SUB_DEV = 2
SUBDOMAINS = 64
NCOARSE = 1024
ITERS = 2


def draw_symmetric(key, count, matrix_order, low_diag, high_diag, spread):

    def single(position):
        sub_key = jax.random.fold_in(key, position)
        key_noise, key_diag = jax.random.split(sub_key)
        noise = jnp.clip(jax.random.normal(key_noise, (matrix_order, matrix_order), jnp.float32), -6.0, 6.0)
        diagonal = jax.random.uniform(key_diag, (matrix_order,), jnp.float32, low_diag, high_diag)
        scale = spread / math.sqrt(2.0 * matrix_order)
        return (noise + noise.T) * scale + jnp.diag(diagonal)
    return lax.map(single, jnp.arange(count))


def draw_inverse_h(key, part):
    base_key = jax.random.fold_in(key, 11)
    return draw_symmetric(base_key, SUBDOMAINS, NS, 5.0, 9.0, 1.0).astype(jnp.bfloat16)


def draw_schur_matrix(key, part):
    base_key = jax.random.fold_in(key, 23)
    return draw_symmetric(base_key, SUBDOMAINS, NS, 5.0, 9.0, 1.0).astype(jnp.bfloat16)


def draw_coarse_inv(key, part):
    base_key = jax.random.fold_in(key, 37)
    return draw_symmetric(base_key, 1, NCOARSE, 1.0, 3.0, 0.4)[0]


def draw_forces(key, part):
    base_key = jax.random.fold_in(key, 41)
    rising = 1.0 + 2.0 * jnp.arange(SUBDOMAINS, dtype=jnp.float32) / max(SUBDOMAINS - 1, 1)
    key_main = jax.random.fold_in(base_key, 0)
    values = jnp.clip(jax.random.normal(key_main, (SUBDOMAINS, LOADS, NS), jnp.float32), -5.0, 5.0)
    return values * rising[:, None, None]


def grid_partners():
    sub_count = SUBDOMAINS // SUB_DEV
    log_sub = int(sub_count).bit_length() - 1
    span_y = 2 ** ((log_sub - 1) // 2)
    span_x = 2 * SUB_DEV
    span_z = sub_count // (2 * span_y)
    sub_ids = np.arange(SUBDOMAINS)
    groups = sub_ids // SUB_DEV
    coord_x = sub_ids % SUB_DEV + SUB_DEV * (groups % 2)
    coord_y = groups // 2 % span_y
    coord_z = groups // (2 * span_y)

    def index_of(cx, cy, cz):
        return ((cz * span_y + cy) * 2 + cx // SUB_DEV) * SUB_DEV + cx % SUB_DEV
    columns = [index_of((coord_x - 1) % span_x, coord_y, coord_z), index_of((coord_x + 1) % span_x, coord_y, coord_z), index_of(coord_x, (coord_y - 1) % span_y, coord_z), index_of(coord_x, (coord_y + 1) % span_y, coord_z), index_of(coord_x, coord_y, (coord_z - 1) % span_z), index_of(coord_x, coord_y, (coord_z + 1) % span_z)]
    return np.stack(columns, axis=1)


def draw_face_perm(key, part):
    base_key = jax.random.fold_in(key, 53)
    total = SUBDOMAINS * FACES * ROWBLK
    keys = jax.random.split(base_key, total)

    def one_perm(sub_key):
        return jax.random.permutation(sub_key, FACEQ)
    base = jax.vmap(one_perm)(keys).reshape(SUBDOMAINS, FACES, ROWBLK, FACEQ).astype(jnp.int32)
    inverse = jnp.argsort(base, axis=-1).astype(jnp.int32)
    partner_ids = grid_partners()
    face_ids = np.arange(FACES)
    partner_inverse = inverse[partner_ids, (face_ids ^ 1)[None, :]]
    odd_face = face_ids % 2 == 1
    result = jnp.where(jnp.asarray(odd_face)[None, :, None, None], partner_inverse, base)
    return result.reshape(SUBDOMAINS, FACES, ROWBLK * FACEQ).astype(jnp.int32)


def draw_corner_rows(key, part):
    base_key = jax.random.fold_in(key, 67)
    nonface = BLOCK - FACES * FACEQ
    keys = jax.random.split(base_key, SUBDOMAINS)

    def one_pick(sub_key):
        return jax.random.permutation(sub_key, ROWBLK * nonface)[:CSLOT]
    picks = jax.vmap(one_pick)(keys).astype(jnp.int32)
    return (picks // nonface * BLOCK + FACES * FACEQ + picks % nonface).astype(jnp.int32)


def draw_corner_count(key, part):
    base_key = jax.random.fold_in(key, 79)
    key_count, key_spot = jax.random.split(base_key)
    counts = jax.random.randint(key_count, (SUBDOMAINS,), max(1, CSLOT // 3), CSLOT + 1).astype(jnp.int32)
    spot = jax.random.randint(key_spot, (), 0, SUBDOMAINS)
    return jnp.where(jnp.arange(SUBDOMAINS) == spot, CSLOT, counts).astype(jnp.int32)


def place_ends(values, own_key, low, top_value):
    shape = values.shape
    spot = [jax.random.randint(jax.random.fold_in(own_key, axis), (), 0, shape[axis]) for axis in range(len(shape))]
    values = values.at[tuple(spot)].set(low)
    longest = shape.index(max(shape))
    spot[longest] = (spot[longest] + 1) % shape[longest]
    return values.at[tuple(spot)].set(top_value)


def setup_inputs(seed: int = 0) -> dict:
    streams_of = jax.random.split(jax.random.key(seed), 9)
    forces = draw_forces(jax.random.fold_in(streams_of[8], 71), 0)
    inverse_h = draw_inverse_h(jax.random.fold_in(streams_of[8], 71), 0)
    schur_matrix = draw_schur_matrix(jax.random.fold_in(streams_of[8], 71), 0)
    coarse_inv = draw_coarse_inv(jax.random.fold_in(streams_of[8], 71), 0)
    face_perm = draw_face_perm(jax.random.fold_in(streams_of[8], 71), 0)
    corner_rows = draw_corner_rows(jax.random.fold_in(streams_of[8], 71), 0)
    corner_ids = place_ends(jax.random.randint(streams_of[6], (SUBDOMAINS, CSLOT), 0, NCOARSE), jax.random.fold_in(streams_of[6], 1), 0, NCOARSE - 1).astype(jnp.int32)
    corner_count = draw_corner_count(jax.random.fold_in(streams_of[8], 71), 0)
    return dict(forces=forces, inverse_h=inverse_h, schur_matrix=schur_matrix, coarse_inv=coarse_inv, face_perm=face_perm, corner_rows=corner_rows, corner_ids=corner_ids, corner_count=corner_count)


HIGHEST = lax.Precision.HIGHEST

def partner_table():
    sub_count = SUBDOMAINS // SUB_DEV
    log_sub = int(sub_count).bit_length() - 1
    span_y = 2 ** ((log_sub - 1) // 2)
    span_x = 2 * SUB_DEV
    span_z = sub_count // (2 * span_y)
    sub_ids = np.arange(SUBDOMAINS)
    groups = sub_ids // SUB_DEV
    coord_x = sub_ids % SUB_DEV + SUB_DEV * (groups % 2)
    coord_y = groups // 2 % span_y
    coord_z = groups // (2 * span_y)

    def index_of(cx, cy, cz):
        return ((cz * span_y + cy) * 2 + cx // SUB_DEV) * SUB_DEV + cx % SUB_DEV
    columns = [index_of((coord_x - 1) % span_x, coord_y, coord_z), index_of((coord_x + 1) % span_x, coord_y, coord_z), index_of(coord_x, (coord_y - 1) % span_y, coord_z), index_of(coord_x, (coord_y + 1) % span_y, coord_z), index_of(coord_x, coord_y, (coord_z - 1) % span_z), index_of(coord_x, coord_y, (coord_z + 1) % span_z)]
    return np.stack(columns, axis=1)

def face_jump(values, face_perm):
    partner_ids = partner_table()
    shaped = values.reshape(SUBDOMAINS, LOADS, ROWBLK, BLOCK)
    face_part = shaped[:, :, :, :FACES * FACEQ].reshape(SUBDOMAINS, LOADS, ROWBLK, FACES, FACEQ)
    order_map = face_perm.reshape(SUBDOMAINS, FACES, ROWBLK, FACEQ)
    jump_list = []
    for face_id in range(FACES):
        own_face = face_part[:, :, :, face_id, :]
        remote = face_part[:, :, :, face_id ^ 1, :][partner_ids[:, face_id]]
        index_map = jnp.broadcast_to(order_map[:, face_id][:, None, :, :], remote.shape)
        picked = jnp.take_along_axis(remote, index_map, axis=3)
        jump_list.append(own_face - picked)
    stacked = jnp.stack(jump_list, axis=3).reshape(SUBDOMAINS, LOADS, ROWBLK, FACES * FACEQ)
    filler = jnp.zeros((SUBDOMAINS, LOADS, ROWBLK, BLOCK - FACES * FACEQ), jnp.float32)
    return jnp.concatenate([stacked, filler], axis=3).reshape(SUBDOMAINS, LOADS, NS)

def matrix_apply(vectors, matrices):
    rounded = vectors.astype(jnp.bfloat16)

    def single(pair):
        vector_one, matrix_one = pair
        return jnp.dot(vector_one.astype(jnp.float32), matrix_one.astype(jnp.float32), preferred_element_type=jnp.float32)
    return lax.map(single, (rounded, matrices))

def columns_at(values_one, row_list):
    return values_one[:, row_list]

def dual_apply(vectors, inverse_h, coarse_inv, corner_rows, corner_ids, corner_count):
    flex = matrix_apply(vectors, inverse_h)
    live_mask = (jnp.arange(CSLOT)[None, :] < corner_count[:, None]).astype(jnp.float32)
    coarse_pick = (corner_ids[:, :, None] == jnp.arange(NCOARSE)[None, None, :]).astype(jnp.float32) * live_mask[:, :, None]
    at_corner = jax.vmap(columns_at)(flex, corner_rows)
    gathered = jnp.einsum('srl,slc->rc', at_corner, coarse_pick, precision=HIGHEST)
    coarse = jnp.dot(gathered, coarse_inv, precision=HIGHEST)
    spread = jnp.einsum('rc,slc->srl', coarse, coarse_pick, precision=HIGHEST).astype(jnp.bfloat16)
    h_rows = inverse_h[jnp.arange(SUBDOMAINS)[:, None], corner_rows]
    correction = jnp.einsum('srl,slk->srk', spread.astype(jnp.float32), h_rows.astype(jnp.float32), precision=HIGHEST)
    return flex + correction

def inner_products(left, right):
    return jnp.einsum('sik,sjk->ij', left, right, precision=HIGHEST)

def combine(vectors, coeffs):
    return jnp.einsum('sjk,ji->sik', vectors, coeffs, precision=HIGHEST)

def chol_solve(matrix, rhs_matrix):
    factor = jnp.linalg.cholesky(matrix)
    return jax.scipy.linalg.cho_solve((factor, True), rhs_matrix)

def reference(forces, inverse_h, schur_matrix, coarse_inv, face_perm, corner_rows, corner_ids, corner_count):

    def dual(vectors):
        return face_jump(dual_apply(vectors, inverse_h, coarse_inv, corner_rows, corner_ids, corner_count), face_perm)

    def precond(vectors):
        return face_jump(matrix_apply(vectors, schur_matrix), face_perm)
    residual = dual(forces)
    multipliers = jnp.zeros_like(residual)
    zvec = precond(residual)
    direction = zvec
    energy = inner_products(residual, zvec)
    for iteration in range(ITERS):
        image_vec = dual(direction)
        curvature = inner_products(direction, image_vec)
        step_size = chol_solve(curvature, energy)
        multipliers = multipliers + combine(direction, step_size)
        residual = residual - combine(image_vec, step_size)
        if iteration + 1 < ITERS:
            zvec = precond(residual)
            energy_next = inner_products(residual, zvec)
            blend = chol_solve(energy, energy_next)
            direction = zvec + combine(direction, blend)
            energy = energy_next
    return (multipliers, residual)
```

```python
import functools

import jax
import jax.numpy as jnp
from jax import lax
from jax.experimental import pallas as pl
from jax.experimental.pallas import tpu as pltpu
from jax.sharding import PartitionSpec as P

MESH = pl.DeviceIdType.MESH
HIGHEST = lax.Precision.HIGHEST
F32 = jnp.float32
BF16 = jnp.bfloat16

NSUB = 32
NROW = 4
LOADS = 16
FACES = 6
FACEQ = 96
WIDE = FACES * 128
BLOCK = 650
NS = 2600
KMAIN = 2560
KFULL = 2688
PART = 640
SPILL = 768
SLOTS = 48

IDS, FORCES, TPART, CFULL, HCORN, XG, CORN, JUMP, ARA, ARB = 0, 1, 2, 3, 4, 5, 9, 12, 17, 21
NSEM = 25


def lanes(shape):
    return lax.broadcasted_iota(jnp.int32, shape, 1)


def dot_nt(a, b, precision=None):
    return lax.dot_general(
        a, b, (((1,), (1,)), ((), ())), precision=precision, preferred_element_type=F32
    )


def dot_nn(a, b, precision=None):
    return lax.dot_general(
        a, b, (((1,), (0,)), ((), ())), precision=precision, preferred_element_type=F32
    )


def dot_tn(a, b, precision=None):
    return lax.dot_general(
        a, b, (((0,), (0,)), ((), ())), precision=precision, preferred_element_type=F32
    )


def lane_gather(x, idx):
    dims = lax.GatherDimensionNumbers(
        offset_dims=(),
        collapsed_slice_dims=(1,),
        start_index_map=(1,),
        operand_batching_dims=(0,),
        start_indices_batching_dims=(0,),
    )
    return lax.gather(
        x, idx[..., None], dims, (1, 1), mode=lax.GatherScatterMode.PROMISE_IN_BOUNDS
    )


def pack_tiles(pieces, shift, count):
    rows = pieces[0].shape[0]
    lane = lanes((rows, 128))
    tiles = [jnp.zeros((rows, 128), F32) for _ in range(count)]
    for f, piece in enumerate(pieces):
        a, b0 = divmod(FACEQ * f, 128)
        b = shift + b0
        if isinstance(b, int) and b == 0:
            rolled = piece
        else:
            rolled = pltpu.roll(piece, b, 1)
        if b0 == 0:
            tiles[a] = tiles[a] + rolled
        else:
            tiles[a] = tiles[a] + jnp.where(lane >= b, rolled, 0.0)
            if a + 1 < count:
                tiles[a + 1] = tiles[a + 1] + jnp.where(lane < b, rolled, 0.0)
    return tiles


def eliminate(m):
    row_id = lax.broadcasted_iota(jnp.int32, (LOADS, 128), 0)
    for k in range(LOADS):
        col = jnp.broadcast_to(m[:, k : k + 1], (LOADS, 128))
        row = jnp.broadcast_to(m[k : k + 1, :], (LOADS, 128))
        pivot = jnp.broadcast_to(col[k : k + 1, :], (LOADS, 128))
        row = row / pivot
        m = jnp.where(row_id == k, row, m - col * row)
    return pltpu.roll(m, 112, 1)


def kernel(
    forces, h_hbm, s_hbm, h_tail, c_own, perm, cr, ids, mult_out, res_out,
    hv, sv, ib, tb, ca, cat, kt, fb, xf, lhs, hco, hcb, hcf, xb, cb, sb, jb, ra, rb, gs, pidx, dv, rv, mv,
    h_sem, s_sem, send, recv,
):
    g = lax.axis_index("sub")
    q = lax.axis_index("row")
    core = lax.rem(g, 2)
    zc = lax.rem(g // 2, 4)
    xc = g // 8

    def dev(x, z, c):
        return (x * 4 + z) * 2 + c

    for f in range(FACES):
        pltpu.make_async_copy(
            h_hbm.at[:, pl.ds(FACEQ * f, FACEQ), :], hv.at[:, pl.ds(128 * f, FACEQ), :], h_sem.at[f]
        ).start()
    for f in range(FACES):
        pltpu.make_async_copy(
            s_hbm.at[:, pl.ds(FACEQ * f, FACEQ), :], sv.at[:, pl.ds(128 * f, FACEQ), :], s_sem.at[f]
        ).start()

    barrier = pltpu.get_barrier_semaphore()

    @pl.loop(1, NSUB)
    def _(k):
        pl.semaphore_signal(
            barrier, inc=1, device_id=(lax.rem(g + k, NSUB), q), device_id_type=MESH
        )

    other = g + 1 - 2 * core
    for k in range(1, NROW):
        far = lax.rem(q + k, NROW)
        pl.semaphore_signal(barrier, inc=1, device_id=(g, far), device_id_type=MESH)
        pl.semaphore_signal(barrier, inc=1, device_id=(other, far), device_id_type=MESH)

    for half in (hv, sv):
        for s in range(2):
            for f in range(FACES):
                half[s, 128 * f + FACEQ : 128 * f + 128, :] = jnp.zeros((32, NS), BF16)
    for i in range(12):
        pidx[i] = jnp.broadcast_to(perm[i : i + 1, :], (LOADS, 128))
    hco[...] = jnp.zeros((128, WIDE), BF16)
    hcf[96:128, :] = jnp.zeros((32, KFULL), BF16)
    kt[96:128, :] = jnp.zeros((32, NSUB * 128), BF16)
    gs[...] = jnp.zeros((32, 128), F32)
    for s in range(2):
        spot = jnp.broadcast_to(cr[s], (SLOTS, KFULL))
        lhs[s, LOADS:, :] = jnp.where(lanes((SLOTS, KFULL)) == spot, 1.0, 0.0).astype(BF16)

    ib[g] = ids[...]
    shift = 10 * q
    lane32 = lanes((32, 128))
    last = jnp.zeros((32, 128), F32)
    for t in range(6):
        now = pltpu.roll(forces[:, 128 * t : 128 * t + 128], shift, 1)
        fb[q, :, 128 * t : 128 * t + 128] = jnp.where(lane32 >= shift, now, last).astype(BF16)
        last = now

    pl.semaphore_wait(barrier, NSUB - 1 + 2 * (NROW - 1))

    def to_plane(src_of, dst, sem):
        @pl.loop(1, NSUB)
        def _(k):
            far = lax.rem(g + k, NSUB)
            pltpu.make_async_remote_copy(
                src_ref=src_of(far),
                dst_ref=dst,
                send_sem=send.at[sem],
                recv_sem=recv.at[sem],
                device_id=(far, q),
                device_id_type=MESH,
            ).start()

    def to_row(ref, sem):
        for k in range(1, NROW):
            pltpu.make_async_remote_copy(
                src_ref=ref,
                dst_ref=ref,
                send_sem=send.at[sem],
                recv_sem=recv.at[sem],
                device_id=(g, lax.rem(q + k, NROW)),
                device_id_type=MESH,
            ).start()

    drains = []

    def arrived(ref, sem):
        pltpu.make_async_copy(ref, ref, recv.at[sem]).wait()
        drains.append((ref, sem))

    to_plane(lambda far: ib.at[g], ib.at[g], IDS)
    to_row(fb.at[q], FORCES)

    arrived(ib.at[pl.ds(0, NSUB - 1)], IDS)

    def pick_columns(far):
        idx = ib[far]
        tile = lax.shift_right_arithmetic(idx, 7)
        lane = lax.bitwise_and(idx, 127)
        total = jnp.zeros((8, 128), F32)
        for v in range(8):
            got = lane_gather(c_own[:, 128 * v : 128 * v + 128], lane)
            total = total + jnp.where(tile == v, got, 0.0)
        return total

    ca[q, g] = pick_columns(g)

    @pl.loop(1, NSUB)
    def _(k):
        far = lax.rem(g + k, NSUB)
        tb[far] = pick_columns(far)
        pltpu.make_async_remote_copy(
            src_ref=tb.at[far],
            dst_ref=ca.at[q, g],
            send_sem=send.at[TPART],
            recv_sem=recv.at[TPART],
            device_id=(far, q),
            device_id_type=MESH,
        ).start()

    def assemble(slots, put):
        for p in range(NROW):
            first = slots[p, :, 0:128]
            if p > 0:
                first = first + slots[p - 1, :, PART:SPILL]
            put(PART * p, first)
            put(PART * p + 128, slots[p, :, 128:PART])
        put(KMAIN, slots[NROW - 1, :, PART:SPILL])

    arrived(fb.at[pl.ds(0, NROW - 1)], FORCES)

    def put_forces(start, value):
        width = value.shape[1]
        xf[:, start : start + width] = value
        lhs[0, :LOADS, start : start + width] = value[:LOADS]
        lhs[1, :LOADS, start : start + width] = value[LOADS:]

    assemble(fb, put_forces)

    for f in range(FACES):
        pltpu.make_async_copy(
            h_hbm.at[:, pl.ds(FACEQ * f, FACEQ), :], hv.at[:, pl.ds(128 * f, FACEQ), :], h_sem.at[f]
        ).wait()

    flex0 = []
    corner_h = jnp.zeros((SLOTS, WIDE), F32)
    corner_t = jnp.zeros((SLOTS, 128), F32)
    for s in range(2):
        prod = dot_nt(lhs[s, :, :KMAIN], hv[s, :, :KMAIN]) + dot_nt(
            lhs[s, :, KMAIN:NS], hv[s, :, KMAIN:NS]
        )
        tail = dot_nt(lhs[s, LOADS:, :KMAIN], h_tail[s, :, :KMAIN]) + dot_nt(
            lhs[s, LOADS:, KMAIN:NS], h_tail[s, :, KMAIN:NS]
        )
        flex0.append(prod[:LOADS])
        corner_h = corner_h + prod[LOADS:]
        corner_t = corner_t + tail
    flex0 = jnp.concatenate(flex0, axis=0)
    rv[...] = flex0
    hco[:SLOTS, :] = corner_h.astype(BF16)
    pieces = [corner_h[:, 128 * f : 128 * f + 128] for f in range(FACES)] + [corner_t]
    for t, tile in enumerate(pack_tiles(pieces, shift, 6)):
        hcb[q, :, 128 * t : 128 * t + 128] = tile.astype(BF16)
    to_row(hcb.at[q], HCORN)

    arrived(ca.at[0, pl.ds(0, NSUB - 1)], TPART)
    to_row(ca.at[q], CFULL)

    arrived(hcb.at[pl.ds(0, NROW - 1)], HCORN)

    def put_corner(start, value):
        width = value.shape[1]
        hcf[:SLOTS, start : start + width] = value
        hcf[SLOTS : 2 * SLOTS, start : start + width] = value

    assemble(hcb, put_corner)

    lane16 = lanes((LOADS, 128))
    first_sub = (lane16 < 24) | ((lane16 >= 48) & (lane16 < 72))
    own_cols = pl.ds(pl.multiple_of(128 * g, 128), 128)

    def corner_send(n, both):
        at = jnp.where(first_sub, both[:LOADS], both[LOADS:])
        high = at.astype(BF16).astype(F32)
        cb[n, :, own_cols] = jnp.where(lane16 < SLOTS, high, at - high).astype(BF16)
        to_plane(lambda far: cb.at[n, :, own_cols], cb.at[n, :, own_cols], CORN + n)

    corner_send(0, dot_nt(xf[...], hcf[...]))

    arrived(ca.at[pl.ds(0, NROW - 1)], CFULL)
    for p in range(NROW):
        for half in range(2):
            block = ca[p, 16 * half : 16 * half + 16].reshape(128, 128)
            spot = (2 * p + half) * 128
            cat[:, spot : spot + 128] = block.T[:SLOTS]

    @pl.loop(0, NSUB)
    def _(far):
        c = ib[far]
        tile = 2 * lax.bitwise_and(lax.shift_right_arithmetic(c, 3), 3) + lax.shift_right_arithmetic(c, 9)
        tile = jnp.where(c < 0, -1, tile)
        lane = 8 * lax.bitwise_and(lax.shift_right_arithmetic(c, 5), 15) + lax.bitwise_and(c, 7)
        cols = pl.ds(pl.multiple_of(128 * far, 128), 128)
        parts = []
        for a in range(SLOTS // 8):
            total = jnp.zeros((8, 128), F32)
            for v in range(8):
                got = lane_gather(cat[8 * a : 8 * a + 8, 128 * v : 128 * v + 128], lane)
                total = total + jnp.where(tile == v, got, 0.0)
            parts.append(total)
        total = jnp.concatenate(parts, axis=0)
        high = total.astype(BF16)
        kt[:SLOTS, cols] = high
        kt[SLOTS : 2 * SLOTS, cols] = (total - high.astype(F32)).astype(BF16)

    def corner_finish(n, flex):
        arrived(cb.at[n, :, pl.ds(0, (NSUB - 1) * 128)], CORN + n)
        spread = dot_nt(cb[n], kt[...])
        spread = spread + pltpu.roll(spread, 128 - SLOTS, 1)
        left = jnp.concatenate(
            [
                jnp.where(lane16 < 24, spread, 0.0),
                jnp.where((lane16 >= 24) & (lane16 < SLOTS), spread, 0.0),
            ],
            axis=0,
        ).astype(BF16)
        return flex + dot_nn(left, hco[...])

    face_targets = {
        2: dev(xc, lax.rem(zc + 3, 4), core),
        3: dev(xc, lax.rem(zc + 1, 4), core),
        4: dev(lax.rem(xc + 3, 4), zc, core),
        5: dev(lax.rem(xc + 1, 4), zc, core),
    }

    def face_of(v, t, f):
        return v[LOADS * t : LOADS * t + LOADS, 128 * f : 128 * f + 128]

    def jump_send(n, v):
        sb[n, 0] = face_of(v, 0, 0)
        sb[n, 1] = face_of(v, 1, 1)
        for f in range(2, FACES):
            for t in range(2):
                sb[n, 2 * f - 2 + t] = face_of(v, t, f)
        moves = [(0, 1, 1, other), (1, 0, 1, other)]
        moves += [(2 * f - 2, 2 * (f ^ 1) - 2, 2, face_targets[f]) for f in range(2, FACES)]
        for src, dst, size, far in moves:
            pltpu.make_async_remote_copy(
                src_ref=sb.at[n, pl.ds(src, size)],
                dst_ref=jb.at[n, pl.ds(dst, size)],
                send_sem=send.at[JUMP + n],
                recv_sem=recv.at[JUMP + n],
                device_id=(far, q),
                device_id_type=MESH,
            ).start()

    def jump_finish(n, v):
        arrived(jb.at[n], JUMP + n)
        subs = []
        for t in range(2):
            out = []
            for f in range(FACES):
                if f < 2:
                    remote = jb[n, f] if f == t else face_of(v, 1 - t, f ^ 1)
                else:
                    remote = jb[n, 2 * f - 2 + t]
                out.append(face_of(v, t, f) - lane_gather(remote, pidx[FACES * t + f]))
            subs.append(jnp.concatenate(out, axis=1))
        return jnp.concatenate(subs, axis=0)

    own_part = pl.ds(pl.multiple_of(PART * q, 128), PART)

    def gather_x(n, x):
        pieces = [x[:, 128 * f : 128 * f + 128] for f in range(FACES)]
        tiles = pack_tiles(pieces, shift, 5)
        xb[n, :, own_part] = jnp.concatenate(tiles, axis=1).astype(BF16)
        to_row(xb.at[n, :, own_part], XG + n)
        arrived(xb.at[n, :, pl.ds(0, 3 * PART)], XG + n)

    def product(n, mat):
        return jnp.concatenate(
            [dot_nt(xb[n, :LOADS, :], mat[0, :, :KMAIN]), dot_nt(xb[n, LOADS:, :], mat[1, :, :KMAIN])],
            axis=0,
        )

    chip_pos = NROW * core + q
    chip_id = g // 2

    def inner_start(n, x, y):
        total = jnp.zeros((32, 32), F32)
        for s in range(2):
            xs, ys = x[LOADS * s : LOADS * s + LOADS], y[LOADS * s : LOADS * s + LOADS]
            total = total + dot_nt(
                jnp.concatenate([xs, ys], axis=0), jnp.concatenate([ys, xs], axis=0), HIGHEST
            )
        gs[:, :32] = total
        plain = jnp.where(lane16 < LOADS, gs[:LOADS], 0.0)
        turned = jnp.where(lane16 < LOADS, pltpu.roll(gs[LOADS:], 112, 1), 0.0)
        sym = plain + turned
        plain = plain + plain
        ra[n, chip_pos] = (
            plain[:8] + pltpu.roll(plain[8:], 16, 1) + pltpu.roll(sym[:8], 32, 1) + pltpu.roll(sym[8:], 48, 1)
        )
        for k in range(1, 2 * NROW):
            pos = lax.rem(chip_pos + k, 2 * NROW)
            pltpu.make_async_remote_copy(
                src_ref=ra.at[n, chip_pos],
                dst_ref=ra.at[n, chip_pos],
                send_sem=send.at[ARA + n],
                recv_sem=recv.at[ARA + n],
                device_id=(2 * chip_id + pos // NROW, lax.rem(pos, NROW)),
                device_id_type=MESH,
            ).start()

    def tree(values):
        while len(values) > 1:
            values = [a + b for a, b in zip(values[::2], values[1::2])]
        return values[0]

    def inner_middle(n):
        arrived(ra.at[n, pl.ds(0, 2 * NROW - 1)], ARA + n)
        rb[n, chip_id] = tree([ra[n, i] for i in range(2 * NROW)])

        @pl.loop(1, NSUB // 2)
        def _(k):
            far = lax.rem(chip_id + k, NSUB // 2)
            pltpu.make_async_remote_copy(
                src_ref=rb.at[n, chip_id],
                dst_ref=rb.at[n, chip_id],
                send_sem=send.at[ARB + n],
                recv_sem=recv.at[ARB + n],
                device_id=(2 * far + core, q),
                device_id_type=MESH,
            ).start()

    def inner_finish(n):
        arrived(rb.at[n, pl.ds(0, NSUB // 2 - 1)], ARB + n)
        total = tree([rb[n, i] for i in range(NSUB // 2)])
        plain = jnp.concatenate([total, pltpu.roll(total, 112, 1)], axis=0)
        sym = jnp.concatenate([pltpu.roll(total, 96, 1), pltpu.roll(total, 80, 1)], axis=0)
        return plain, sym

    def solve(a, b):
        return eliminate(
            jnp.where(lane16 < LOADS, a, jnp.where(lane16 < 2 * LOADS, pltpu.roll(b, 16, 1), 0.0))
        )

    def combine(x, coeffs):
        small = coeffs[:, :LOADS]
        return jnp.concatenate(
            [dot_tn(small, x[:LOADS], HIGHEST), dot_tn(small, x[LOADS:], HIGHEST)], axis=0
        )

    v = corner_finish(0, rv[...])
    jump_send(0, v)
    rv[...] = jump_finish(0, v)

    gather_x(0, rv[...])
    for f in range(FACES):
        pltpu.make_async_copy(
            s_hbm.at[:, pl.ds(FACEQ * f, FACEQ), :], sv.at[:, pl.ds(128 * f, FACEQ), :], s_sem.at[f]
        ).wait()
    y = product(0, sv)
    jump_send(1, y)
    inner_start(0, rv[...], y)
    dv[...] = jump_finish(1, y)

    gather_x(1, dv[...])
    corner_send(1, dot_nt(xb[1], hcf[:, :KMAIN]))
    inner_middle(0)
    flex = product(1, hv)
    v = corner_finish(1, flex)
    inner_start(1, dv[...], v)
    jump_send(2, v)
    energy, energy_sym = inner_finish(0)
    inner_middle(1)
    image = jump_finish(2, v)
    unused, curvature = inner_finish(1)
    step = solve(curvature, energy)
    rv[...] = rv[...] - combine(image, step)
    gather_x(2, rv[...])
    y = product(2, sv)
    inner_start(2, rv[...], y)
    jump_send(3, y)
    mv[...] = combine(dv[...], step)
    inner_middle(2)
    zvec = jump_finish(3, y)
    energy_next, unused = inner_finish(2)
    blend = solve(energy_sym, energy_next)
    dv[...] = zvec + combine(dv[...], blend)

    gather_x(3, dv[...])
    corner_send(2, dot_nt(xb[3], hcf[:, :KMAIN]))
    flex = product(3, hv)
    v = corner_finish(2, flex)
    inner_start(3, dv[...], v)
    jump_send(4, v)
    inner_middle(3)
    image = jump_finish(4, v)
    unused, curvature = inner_finish(3)
    step = solve(curvature, energy_next)

    def put_out(ref, value):
        tiles = pack_tiles([value[:, 128 * f : 128 * f + 128] for f in range(FACES)], 0, 5)
        for s in range(2):
            for t in range(5):
                ref[s, :, 128 * t : 128 * t + 128] = tiles[t][LOADS * s : LOADS * s + LOADS]
            ref[s, :, PART:BLOCK] = jnp.zeros((LOADS, BLOCK - PART), F32)

    put_out(mult_out, mv[...] + combine(dv[...], step))
    put_out(res_out, rv[...] - combine(image, step))

    for ref, sem in drains:
        pltpu.make_async_copy(ref, ref, send.at[sem]).wait()


def body(
    forces, inverse_h, schur_matrix, coarse_inv, face_perm, corner_rows, corner_ids, corner_count
):
    fpad = jnp.pad(forces, ((0, 0), (0, 0), (0, SPILL - BLOCK))).reshape(2 * LOADS, SPILL)
    h_tail = jnp.pad(inverse_h[:, FACES * FACEQ :, :], ((0, 0), (0, 128 - (BLOCK - FACES * FACEQ)), (0, 0)))
    perm = jnp.pad(face_perm, ((0, 0), (0, 0), (0, 128 - FACEQ)), constant_values=127).reshape(12, 128)
    none = jnp.full((24,), -1, jnp.int32)
    cr = jnp.stack(
        [jnp.concatenate([corner_rows[0], none]), jnp.concatenate([none, corner_rows[1]])]
    )[..., None]
    live = jnp.where(jnp.arange(24)[None, :] < corner_count[:, None], corner_ids, -1).reshape(SLOTS)
    ids = jnp.concatenate([live, live, jnp.full((32,), -1, jnp.int32)])
    ids = jnp.broadcast_to(ids[None, :], (8, 128))

    vmem = pl.BlockSpec(memory_space=pltpu.VMEM)
    hbm = pl.BlockSpec(memory_space=pl.ANY)
    out = jax.ShapeDtypeStruct((2, LOADS, BLOCK), F32)
    return pl.pallas_call(
        kernel,
        out_shape=(out, out),
        in_specs=[vmem, hbm, hbm, vmem, vmem, vmem, vmem, vmem],
        out_specs=(vmem, vmem),
        scratch_shapes=[
            pltpu.VMEM((2, WIDE, NS), BF16),
            pltpu.VMEM((2, WIDE, NS), BF16),
            pltpu.VMEM((NSUB, 8, 128), jnp.int32),
            pltpu.VMEM((NSUB, 8, 128), F32),
            pltpu.VMEM((NROW, NSUB, 8, 128), F32),
            pltpu.VMEM((SLOTS, 1024), F32),
            pltpu.VMEM((128, NSUB * 128), BF16),
            pltpu.VMEM((NROW, 32, SPILL), BF16),
            pltpu.VMEM((32, KFULL), BF16),
            pltpu.VMEM((2, LOADS + SLOTS, KFULL), BF16),
            pltpu.VMEM((128, WIDE), BF16),
            pltpu.VMEM((NROW, SLOTS, SPILL), BF16),
            pltpu.VMEM((128, KFULL), BF16),
            pltpu.VMEM((4, 32, KMAIN), BF16),
            pltpu.VMEM((3, LOADS, NSUB * 128), BF16),
            pltpu.VMEM((5, 10, LOADS, 128), F32),
            pltpu.VMEM((5, 10, LOADS, 128), F32),
            pltpu.VMEM((4, 2 * NROW, 8, 128), F32),
            pltpu.VMEM((4, NSUB // 2, 8, 128), F32),
            pltpu.VMEM((32, 128), F32),
            pltpu.VMEM((12, LOADS, 128), jnp.int32),
            pltpu.VMEM((32, WIDE), F32),
            pltpu.VMEM((32, WIDE), F32),
            pltpu.VMEM((32, WIDE), F32),
            pltpu.SemaphoreType.DMA((FACES,)),
            pltpu.SemaphoreType.DMA((FACES,)),
            pltpu.SemaphoreType.DMA((NSEM,)),
            pltpu.SemaphoreType.DMA((NSEM,)),
        ],
        compiler_params=pltpu.CompilerParams(
            collective_id=0, has_side_effects=True, vmem_limit_bytes=48 * 1024 * 1024
        ),
    )(fpad, inverse_h, schur_matrix, h_tail, coarse_inv, perm, cr, ids)


def solution(mesh):
    in_specs = (
        P("sub", None, "row"),
        P("sub", "row", None),
        P("sub", "row", None),
        P(("sub", "row"), None),
        P("sub", None, "row"),
        P("sub", None),
        P("sub", None),
        P("sub"),
    )
    out_specs = (P("sub", None, "row"), P("sub", None, "row"))
    return jax.shard_map(body, mesh=mesh, in_specs=in_specs, out_specs=out_specs, check_vma=False)
```

```python
import functools

import jax
import jax.numpy as jnp
from jax import lax
from jax.experimental import pallas as pl
from jax.experimental.pallas import tpu as pltpu
from jax.sharding import PartitionSpec as P

MESH = pl.DeviceIdType.MESH
HIGHEST = lax.Precision.HIGHEST
F32 = jnp.float32
BF16 = jnp.bfloat16

NSUB = 32
NROW = 4
LOADS = 16
FACES = 6
FACEQ = 96
WIDE = FACES * 128
BLOCK = 650
NS = 2600
KMAIN = 2560
KFULL = 2688
PART = 640
SPILL = 768
SLOTS = 48

IDS, FORCES, TPART, CFULL, HCORN, XG, CORN, JUMP, ARA, ARB = 0, 1, 2, 3, 4, 5, 9, 12, 17, 21
XL = 25
NSEM = 29


def lanes(shape):
    return lax.broadcasted_iota(jnp.int32, shape, 1)


def dot_nt(a, b, precision=None):
    return lax.dot_general(
        a, b, (((1,), (1,)), ((), ())), precision=precision, preferred_element_type=F32
    )


def dot_nn(a, b, precision=None):
    return lax.dot_general(
        a, b, (((1,), (0,)), ((), ())), precision=precision, preferred_element_type=F32
    )


def dot_tn(a, b, precision=None):
    return lax.dot_general(
        a, b, (((0,), (0,)), ((), ())), precision=precision, preferred_element_type=F32
    )


def lane_gather(x, idx):
    dims = lax.GatherDimensionNumbers(
        offset_dims=(),
        collapsed_slice_dims=(1,),
        start_index_map=(1,),
        operand_batching_dims=(0,),
        start_indices_batching_dims=(0,),
    )
    return lax.gather(
        x, idx[..., None], dims, (1, 1), mode=lax.GatherScatterMode.PROMISE_IN_BOUNDS
    )


def pack_tiles(pieces, shift, count):
    rows = pieces[0].shape[0]
    lane = lanes((rows, 128))
    tiles = [jnp.zeros((rows, 128), F32) for _ in range(count)]
    for f, piece in enumerate(pieces):
        a, b0 = divmod(FACEQ * f, 128)
        b = shift + b0
        if isinstance(b, int) and b == 0:
            rolled = piece
        else:
            rolled = pltpu.roll(piece, b, 1)
        if b0 == 0:
            tiles[a] = tiles[a] + rolled
        else:
            tiles[a] = tiles[a] + jnp.where(lane >= b, rolled, 0.0)
            if a + 1 < count:
                tiles[a + 1] = tiles[a + 1] + jnp.where(lane < b, rolled, 0.0)
    return tiles


def eliminate(m):
    wide = (LOADS, 128)
    row_id = lax.broadcasted_iota(jnp.int32, wide, 0)
    cols = [jnp.broadcast_to(m[:, k : k + 1], wide) for k in range(LOADS)]
    for k in range(LOADS):
        scale = 1.0 / jnp.broadcast_to(cols[k][k : k + 1, :], wide)

        def step(x):
            row = jnp.broadcast_to(x[k : k + 1, :], wide) * scale
            return jnp.where(row_id == k, row, x - cols[k] * row)

        m = step(m)
        for j in range(k + 1, LOADS):
            cols[j] = step(cols[j])
    return pltpu.roll(m, 112, 1)


def kernel(
    forces_in, h_hbm, s_hbm, c_in, perm_in, rows_in, ids_in, count_in, mult_out, res_out,
    forces, c_own, perm, corner_rows, corner_ids, count,
    raw_h, raw_s, hv, sv, ht, ib, tb, ca, cat, kt, fb, ft, xf, oh, hco, hcb, hcf, xb, xl, xw, cb, sb, jb, ra, rb, gs, pidx,
    small, dv, rv, mv, in_sem, h_sem, s_sem, send, recv,
):
    g = lax.axis_index("sub")
    q = lax.axis_index("row")
    core = lax.rem(g, 2)
    zc = lax.rem(g // 2, 4)
    xc = g // 8

    def dev(x, z, c):
        return (x * 4 + z) * 2 + c

    def load(src, dst, sem, f):
        size = FACEQ if f < FACES else BLOCK - FACES * FACEQ
        rows = pl.ds(FACEQ * f, size)
        return pltpu.make_async_copy(src.at[rows], dst.at[rows], sem.at[f])

    inputs = [
        pltpu.make_async_copy(src, dst, in_sem.at[i])
        for i, (src, dst) in enumerate(
            [(ids_in, corner_ids), (count_in, count), (forces_in, forces), (rows_in, corner_rows)]
            + [(c_in, c_own), (perm_in, perm)]
        )
    ]
    for copy in inputs:
        copy.start()
    for f in range(FACES + 1):
        load(h_hbm, raw_h, h_sem, f).start()

    barrier = pltpu.get_barrier_semaphore()

    @pl.loop(1, NSUB)
    def _(k):
        pl.semaphore_signal(
            barrier, inc=1, device_id=(lax.rem(g + k, NSUB), q), device_id_type=MESH
        )

    other = g + 1 - 2 * core
    for k in range(1, NROW):
        far = lax.rem(q + k, NROW)
        pl.semaphore_signal(barrier, inc=1, device_id=(g, far), device_id_type=MESH)
        pl.semaphore_signal(barrier, inc=1, device_id=(other, far), device_id_type=MESH)

    for f in range(FACES):
        load(s_hbm, raw_s, s_sem, f).start()

    for copy in inputs:
        copy.wait()
    lane8 = lanes((8, 128))

    def slot_row(ref, first, second):
        small[...] = jnp.full((8, 128), -1, jnp.int32)
        small[0:2, 0:24] = ref[...]
        top = jnp.broadcast_to(small[0:1, :], (8, 128))
        low = pltpu.roll(jnp.broadcast_to(small[1:2, :], (8, 128)), 24, 1)
        out = jnp.where(lane8 < first, top, -1)
        return jnp.where((lane8 >= 24) & (lane8 < 24 + second), low, out)

    live = slot_row(corner_ids, jnp.minimum(count[0], 24), jnp.minimum(count[1], 24))
    both = pltpu.roll(live, SLOTS, 1)
    ib[g] = jnp.where(lane8 < SLOTS, live, jnp.where(lane8 < 2 * SLOTS, both, -1))

    shift = 10 * q
    lane32 = lanes((32, 128))
    last = jnp.zeros((32, 128), F32)
    ft[...] = last
    for s in range(2):
        ft[LOADS * s : LOADS * s + LOADS, 0 : BLOCK - PART] = forces[s, :, PART:BLOCK]
    for t in range(6):
        if t < 5:
            now = jnp.concatenate([forces[s, :, 128 * t : 128 * t + 128] for s in range(2)], axis=0)
        else:
            now = ft[...]
        now = pltpu.roll(now, shift, 1)
        fb[q, :, 128 * t : 128 * t + 128] = jnp.where(lane32 >= shift, now, last).astype(BF16)
        last = now

    rows = slot_row(corner_rows, 24, 24).astype(F32)
    spot = jnp.broadcast_to(rows[0:1, :], (128, 128)).T[:SLOTS].astype(jnp.int32)
    lane48 = lanes((SLOTS, 128))
    upper = lax.broadcasted_iota(jnp.int32, (SLOTS, 128), 0) < 24
    for t in range(KFULL // 128):
        hit = jnp.where(lane48 + 128 * t == spot, 1.0, 0.0)
        oh[0, :, 128 * t : 128 * t + 128] = jnp.where(upper, hit, 0.0).astype(BF16)
        oh[1, :, 128 * t : 128 * t + 128] = jnp.where(upper, 0.0, hit).astype(BF16)
    for s in range(2):
        for f in range(FACES):
            hv[s, 128 * f + FACEQ : 128 * f + 128, :] = jnp.zeros((32, NS), BF16)
    hco[...] = jnp.zeros((128, WIDE), BF16)

    def split(raw, start, dst, at, count):
        @pl.loop(0, count)
        def _(i):
            pair = jnp.swapaxes(raw[pl.ds(start + 16 * i, 16)], 0, 1)
            for s in range(2):
                dst[s, pl.ds(pl.multiple_of(at + 16 * i, 16), 16), :] = pair[s]

    for f in range(FACES):
        load(h_hbm, raw_h, h_sem, f).wait()
        split(raw_h, FACEQ * f, hv, 128 * f, FACEQ // 16)
    load(h_hbm, raw_h, h_sem, FACES).wait()
    split(raw_h, FACEQ * FACES, ht, 0, 5)

    pl.semaphore_wait(barrier, NSUB - 1 + 2 * (NROW - 1))

    def to_plane(src_of, dst, sem):
        @pl.loop(1, NSUB)
        def _(k):
            far = lax.rem(g + k, NSUB)
            pltpu.make_async_remote_copy(
                src_ref=src_of(far),
                dst_ref=dst,
                send_sem=send.at[sem],
                recv_sem=recv.at[sem],
                device_id=(far, q),
                device_id_type=MESH,
            ).start()

    def to_row(ref, sem):
        for k in range(1, NROW):
            pltpu.make_async_remote_copy(
                src_ref=ref,
                dst_ref=ref,
                send_sem=send.at[sem],
                recv_sem=recv.at[sem],
                device_id=(g, lax.rem(q + k, NROW)),
                device_id_type=MESH,
            ).start()

    drains = []

    def arrived(ref, sem):
        pltpu.make_async_copy(ref, ref, recv.at[sem]).wait()
        drains.append((ref, sem))

    to_plane(lambda far: ib.at[g], ib.at[g], IDS)
    to_row(fb.at[q], FORCES)

    corner_h = jnp.zeros((SLOTS, WIDE), F32)
    corner_t = jnp.zeros((SLOTS, 128), F32)
    for s in range(2):
        corner_h = corner_h + dot_nt(oh[s, :, :KMAIN], hv[s, :, :KMAIN])
        corner_h = corner_h + dot_nt(oh[s, :, KMAIN:NS], hv[s, :, KMAIN:NS])
        corner_t = corner_t + dot_nt(oh[s, :, :KMAIN], ht[s, :, :KMAIN])
        corner_t = corner_t + dot_nt(oh[s, :, KMAIN:NS], ht[s, :, KMAIN:NS])
    corner_t = jnp.where(lane48 < BLOCK - FACES * FACEQ, corner_t, 0.0)
    hco[:SLOTS, :] = corner_h.astype(BF16)
    pieces = [corner_h[:, 128 * f : 128 * f + 128] for f in range(FACES)] + [corner_t]
    for t, tile in enumerate(pack_tiles(pieces, shift, 6)):
        hcb[q, :, 128 * t : 128 * t + 128] = tile.astype(BF16)
    to_row(hcb.at[q], HCORN)

    arrived(ib.at[pl.ds(0, NSUB - 1)], IDS)

    def pick_columns(far):
        idx = ib[far]
        tile = lax.shift_right_arithmetic(idx, 7)
        lane = lax.bitwise_and(idx, 127)
        total = jnp.zeros((8, 128), F32)
        for v in range(8):
            got = lane_gather(c_own[:, 128 * v : 128 * v + 128], lane)
            total = total + jnp.where(tile == v, got, 0.0)
        return total

    ca[g] = pick_columns(g)

    @pl.loop(1, NSUB)
    def _(k):
        far = lax.rem(g + k, NSUB)
        tb[far] = pick_columns(far)
        pltpu.make_async_remote_copy(
            src_ref=tb.at[far],
            dst_ref=ca.at[g],
            send_sem=send.at[TPART],
            recv_sem=recv.at[TPART],
            device_id=(far, q),
            device_id_type=MESH,
        ).start()

    def assemble(slots, put):
        for p in range(NROW):
            first = slots[p, :, 0:128]
            if p > 0:
                first = first + slots[p - 1, :, PART:SPILL]
            put(PART * p, first)
            put(PART * p + 128, slots[p, :, 128:PART])
        put(KMAIN, slots[NROW - 1, :, PART:SPILL])

    arrived(fb.at[pl.ds(0, NROW - 1)], FORCES)

    def put_forces(start, value):
        xf[:, start : start + value.shape[1]] = value

    assemble(fb, put_forces)

    arrived(hcb.at[pl.ds(0, NROW - 1)], HCORN)
    hcf[96:128, :] = jnp.zeros((32, KFULL), BF16)

    def put_corner(start, value):
        width = value.shape[1]
        hcf[:SLOTS, start : start + width] = value
        hcf[SLOTS : 2 * SLOTS, start : start + width] = value

    assemble(hcb, put_corner)

    lane16 = lanes((LOADS, 128))
    first_sub = (lane16 < 24) | ((lane16 >= 48) & (lane16 < 72))
    own_cols = pl.ds(pl.multiple_of(128 * g, 128), 128)

    def corner_send(n, both):
        at = jnp.where(first_sub, both[:LOADS], both[LOADS:])
        high = at.astype(BF16).astype(F32)
        cb[n, :, own_cols] = jnp.where(lane16 < SLOTS, high, at - high).astype(BF16)
        to_plane(lambda far: cb.at[n, :, own_cols], cb.at[n, :, own_cols], CORN + n)

    corner_send(0, dot_nt(xf[...], hcf[...]))

    arrived(ca.at[pl.ds(0, NSUB - 1)], TPART)
    for half in range(2):
        block = ca[16 * half : 16 * half + 16].reshape(128, 128)
        cat[q, :, 128 * half : 128 * half + 128] = block.T[:SLOTS]
    to_row(cat.at[q], CFULL)

    for s in range(2):
        rv[LOADS * s : LOADS * s + LOADS, :] = dot_nt(
            xf[LOADS * s : LOADS * s + LOADS, :KMAIN], hv[s, :, :KMAIN]
        ) + dot_nt(xf[LOADS * s : LOADS * s + LOADS, KMAIN:NS], hv[s, :, KMAIN:NS])

    for f in range(FACES):
        for t in range(2):
            pidx[FACES * t + f] = jnp.full((LOADS, 128), 127, jnp.int32)
            pidx[FACES * t + f, :, :FACEQ] = jnp.broadcast_to(perm[f, t : t + 1, :], (LOADS, FACEQ))
    kt[96:128, :] = jnp.zeros((32, NSUB * 128), BF16)
    gs[...] = jnp.zeros((32, 128), F32)
    for s in range(2):
        for f in range(FACES):
            sv[s, 128 * f + FACEQ : 128 * f + 128, :] = jnp.zeros((32, NS), BF16)
    for f in range(FACES):
        load(s_hbm, raw_s, s_sem, f).wait()
        split(raw_s, FACEQ * f, sv, 128 * f, FACEQ // 16)

    arrived(cat.at[pl.ds(0, NROW - 1)], CFULL)

    slot_lane = lanes((SLOTS, 128))

    @pl.loop(0, NSUB // 2)
    def _(pair):
        c = jnp.where(lane8 < SLOTS, ib[2 * pair], ib[2 * pair + 1])
        tile = 2 * lax.bitwise_and(lax.shift_right_arithmetic(c, 3), 3) + lax.shift_right_arithmetic(c, 9)
        tile = jnp.where(c < 0, -1, tile)
        lane = 8 * lax.bitwise_and(lax.shift_right_arithmetic(c, 5), 15) + lax.bitwise_and(c, 7)
        parts = []
        for a in range(SLOTS // 8):
            total = jnp.zeros((8, 128), F32)
            for v in range(8):
                got = lane_gather(cat[v // 2, 8 * a : 8 * a + 8, 128 * (v % 2) : 128 * (v % 2) + 128], lane)
                total = total + jnp.where(tile == v, got, 0.0)
            parts.append(total)
        total = jnp.concatenate(parts, axis=0)
        first = jnp.where(slot_lane < SLOTS, total, pltpu.roll(total, SLOTS, 1))
        second = jnp.where(slot_lane < SLOTS, pltpu.roll(total, 128 - SLOTS, 1), total)
        for i, part in enumerate((first, second)):
            part = jnp.where(slot_lane < 2 * SLOTS, part, 0.0)
            high = part.astype(BF16)
            cols = pl.ds(pl.multiple_of(256 * pair + 128 * i, 128), 128)
            kt[:SLOTS, cols] = high
            kt[SLOTS : 2 * SLOTS, cols] = (part - high.astype(F32)).astype(BF16)

    def corner_finish(n, flex):
        arrived(cb.at[n, :, pl.ds(0, (NSUB - 1) * 128)], CORN + n)
        spread = dot_nt(cb[n], kt[...])
        spread = spread + pltpu.roll(spread, 128 - SLOTS, 1)
        left = jnp.concatenate(
            [
                jnp.where(lane16 < 24, spread, 0.0),
                jnp.where((lane16 >= 24) & (lane16 < SLOTS), spread, 0.0),
            ],
            axis=0,
        ).astype(BF16)
        return flex + dot_nn(left, hco[...])

    face_targets = {
        2: dev(xc, lax.rem(zc + 3, 4), core),
        3: dev(xc, lax.rem(zc + 1, 4), core),
        4: dev(lax.rem(xc + 3, 4), zc, core),
        5: dev(lax.rem(xc + 1, 4), zc, core),
    }

    def face_of(v, t, f):
        return v[LOADS * t : LOADS * t + LOADS, 128 * f : 128 * f + 128]

    def jump_send(n, v):
        sb[n, 0] = face_of(v, 0, 0)
        sb[n, 1] = face_of(v, 1, 1)
        for f in range(2, FACES):
            for t in range(2):
                sb[n, 2 * f - 2 + t] = face_of(v, t, f)
        moves = [(0, 1, 1, other), (1, 0, 1, other)]
        moves += [(2 * f - 2, 2 * (f ^ 1) - 2, 2, face_targets[f]) for f in range(2, FACES)]
        for src, dst, size, far in moves:
            pltpu.make_async_remote_copy(
                src_ref=sb.at[n, pl.ds(src, size)],
                dst_ref=jb.at[n, pl.ds(dst, size)],
                send_sem=send.at[JUMP + n],
                recv_sem=recv.at[JUMP + n],
                device_id=(far, q),
                device_id_type=MESH,
            ).start()

    def jump_finish(n, v):
        arrived(jb.at[n], JUMP + n)
        subs = []
        for t in range(2):
            out = []
            for f in range(FACES):
                if f < 2:
                    remote = jb[n, f] if f == t else face_of(v, 1 - t, f ^ 1)
                else:
                    remote = jb[n, 2 * f - 2 + t]
                out.append(face_of(v, t, f) - lane_gather(remote, pidx[FACES * t + f]))
            subs.append(jnp.concatenate(out, axis=1))
        return jnp.concatenate(subs, axis=0)

    own_part = pl.ds(pl.multiple_of(PART * q, 128), PART)

    def gather_send(n, x):
        pieces = [x[:, 128 * f : 128 * f + 128] for f in range(FACES)]
        whole = jnp.concatenate(pack_tiles(pieces, shift, 5), axis=1)
        high = whole.astype(BF16)
        xb[n, :, own_part] = high
        to_row(xb.at[n, :, own_part], XG + n)
        xl[n, :, own_part] = (whole - high.astype(F32)).astype(BF16)
        to_row(xl.at[n, :, own_part], XL + n)

    def gather_high(n):
        arrived(xb.at[n, :, pl.ds(0, 3 * PART)], XG + n)

    def gather_low(n):
        arrived(xl.at[n, :, pl.ds(0, 3 * PART)], XL + n)

    def full(n):
        return xb[n].astype(F32) + xl[n].astype(F32)

    def product(x, mat):
        return jnp.concatenate(
            [dot_nt(x[:LOADS, :], mat[0, :, :KMAIN]), dot_nt(x[LOADS:, :], mat[1, :, :KMAIN])],
            axis=0,
        )

    chip_pos = NROW * core + q
    chip_id = g // 2

    def inner_start(n, x, y):
        total = jnp.zeros((32, 32), F32)
        for s in range(2):
            xs, ys = x[LOADS * s : LOADS * s + LOADS], y[LOADS * s : LOADS * s + LOADS]
            total = total + dot_nt(
                jnp.concatenate([xs, ys], axis=0), jnp.concatenate([ys, xs], axis=0), HIGHEST
            )
        gs[:, :32] = total
        plain = jnp.where(lane16 < LOADS, gs[:LOADS], 0.0)
        turned = jnp.where(lane16 < LOADS, pltpu.roll(gs[LOADS:], 112, 1), 0.0)
        sym = plain + turned
        plain = plain + plain
        ra[n, chip_pos] = (
            plain[:8] + pltpu.roll(plain[8:], 16, 1) + pltpu.roll(sym[:8], 32, 1) + pltpu.roll(sym[8:], 48, 1)
        )
        for k in range(1, 2 * NROW):
            pos = lax.rem(chip_pos + k, 2 * NROW)
            pltpu.make_async_remote_copy(
                src_ref=ra.at[n, chip_pos],
                dst_ref=ra.at[n, chip_pos],
                send_sem=send.at[ARA + n],
                recv_sem=recv.at[ARA + n],
                device_id=(2 * chip_id + pos // NROW, lax.rem(pos, NROW)),
                device_id_type=MESH,
            ).start()

    def tree(values):
        while len(values) > 1:
            values = [a + b for a, b in zip(values[::2], values[1::2])]
        return values[0]

    def inner_middle(n):
        arrived(ra.at[n, pl.ds(0, 2 * NROW - 1)], ARA + n)
        rb[n, chip_id] = tree([ra[n, i] for i in range(2 * NROW)])

        @pl.loop(1, NSUB // 2)
        def _(k):
            far = lax.rem(chip_id + k, NSUB // 2)
            pltpu.make_async_remote_copy(
                src_ref=rb.at[n, chip_id],
                dst_ref=rb.at[n, chip_id],
                send_sem=send.at[ARB + n],
                recv_sem=recv.at[ARB + n],
                device_id=(2 * far + core, q),
                device_id_type=MESH,
            ).start()

    def inner_finish(n):
        arrived(rb.at[n, pl.ds(0, NSUB // 2 - 1)], ARB + n)
        total = tree([rb[n, i] for i in range(NSUB // 2)])
        plain = jnp.concatenate([total, pltpu.roll(total, 112, 1)], axis=0)
        sym = jnp.concatenate([pltpu.roll(total, 96, 1), pltpu.roll(total, 80, 1)], axis=0)
        return plain, sym

    def solve(a, b):
        return eliminate(
            jnp.where(lane16 < LOADS, a, jnp.where(lane16 < 2 * LOADS, pltpu.roll(b, 16, 1), 0.0))
        )

    def combine(x, coeffs):
        small = coeffs[:, :LOADS]
        return jnp.concatenate(
            [dot_tn(small, x[:LOADS], HIGHEST), dot_tn(small, x[LOADS:], HIGHEST)], axis=0
        )

    v = corner_finish(0, rv[...])
    jump_send(0, v)
    rv[...] = jump_finish(0, v)

    gather_send(0, rv[...])
    gather_high(0)
    y = product(xb.at[0], sv)
    jump_send(1, y)
    inner_start(0, rv[...], y)
    dv[...] = jump_finish(1, y)

    gather_send(1, dv[...])
    gather_low(0)
    gather_high(1)
    corner_send(1, dot_nt(xb[1], hcf[:, :KMAIN]))
    inner_middle(0)
    flex = product(xb.at[1], hv)
    v = corner_finish(1, flex)
    jump_send(2, v)
    inner_start(1, dv[...], v)
    gather_low(1)
    energy, energy_sym = inner_finish(0)
    row16 = lax.broadcasted_iota(jnp.int32, (LOADS, 128), 0)
    energy_inv = solve(energy_sym, jnp.where(row16 == lane16, 1.0, 0.0))
    image = jump_finish(2, v)
    gather_send(2, image)
    inner_middle(1)
    unused, curvature = inner_finish(1)
    step = solve(curvature, energy)
    rv[...] = rv[...] - combine(image, step)
    gather_high(2)
    gather_low(2)
    xw[0] = (full(0) - combine(full(2), step)).astype(BF16)
    y = product(xw.at[0], sv)
    jump_send(3, y)
    inner_start(2, rv[...], y)
    mv[...] = combine(dv[...], step)
    zvec = jump_finish(3, y)
    gather_send(3, zvec)
    inner_middle(2)
    energy_next, unused = inner_finish(2)
    blend = dot_nn(energy_inv[:, :LOADS], energy_next[:, :LOADS], HIGHEST)
    dv[...] = zvec + combine(dv[...], blend)

    gather_high(3)
    gather_low(3)
    xw[1] = (full(3) + combine(full(1), blend)).astype(BF16)
    corner_send(2, dot_nt(xw[1], hcf[:, :KMAIN]))
    flex = product(xw.at[1], hv)
    v = corner_finish(2, flex)
    inner_start(3, dv[...], v)
    jump_send(4, v)
    inner_middle(3)
    image = jump_finish(4, v)
    unused, curvature = inner_finish(3)
    step = solve(curvature, energy_next)

    def put_out(ref, value):
        tiles = pack_tiles([value[:, 128 * f : 128 * f + 128] for f in range(FACES)], 0, 5)
        for s in range(2):
            for t in range(5):
                ref[s, :, 128 * t : 128 * t + 128] = tiles[t][LOADS * s : LOADS * s + LOADS]
            ref[s, :, PART:BLOCK] = jnp.zeros((LOADS, BLOCK - PART), F32)

    put_out(mult_out, mv[...] + combine(dv[...], step))
    put_out(res_out, rv[...] - combine(image, step))

    for ref, sem in drains:
        pltpu.make_async_copy(ref, ref, send.at[sem]).wait()


def body(
    forces, inverse_h, schur_matrix, coarse_inv, face_perm, corner_rows, corner_ids, corner_count
):
    h = jnp.transpose(inverse_h, (1, 0, 2))
    schur = jnp.transpose(schur_matrix, (1, 0, 2))
    perm = jnp.transpose(face_perm, (1, 0, 2))
    vmem = pl.BlockSpec(memory_space=pltpu.VMEM)
    hbm = pl.BlockSpec(memory_space=pltpu.MemorySpace.HBM)
    out = jax.ShapeDtypeStruct((2, LOADS, BLOCK), F32)
    return pl.pallas_call(
        kernel,
        out_shape=(out, out),
        in_specs=[hbm] * 8,
        out_specs=(vmem, vmem),
        scratch_shapes=[
            pltpu.VMEM((2, LOADS, BLOCK), F32),
            pltpu.VMEM((8, 1024), F32),
            pltpu.VMEM((FACES, 2, FACEQ), jnp.int32),
            pltpu.VMEM((2, 24), jnp.int32),
            pltpu.VMEM((2, 24), jnp.int32),
            pltpu.SMEM((2,), jnp.int32),
            pltpu.VMEM((656, 2, NS), BF16),
            pltpu.VMEM((FACES * FACEQ, 2, NS), BF16),
            pltpu.VMEM((2, WIDE, NS), BF16),
            pltpu.VMEM((2, WIDE, NS), BF16),
            pltpu.VMEM((2, 128, NS), BF16),
            pltpu.VMEM((NSUB, 8, 128), jnp.int32),
            pltpu.VMEM((NSUB, 8, 128), F32),
            pltpu.VMEM((NSUB, 8, 128), F32),
            pltpu.VMEM((NROW, SLOTS, 256), F32),
            pltpu.VMEM((128, NSUB * 128), BF16),
            pltpu.VMEM((NROW, 32, SPILL), BF16),
            pltpu.VMEM((32, 128), F32),
            pltpu.VMEM((32, KFULL), BF16),
            pltpu.VMEM((2, SLOTS, KFULL), BF16),
            pltpu.VMEM((128, WIDE), BF16),
            pltpu.VMEM((NROW, SLOTS, SPILL), BF16),
            pltpu.VMEM((128, KFULL), BF16),
            pltpu.VMEM((4, 32, KMAIN), BF16),
            pltpu.VMEM((4, 32, KMAIN), BF16),
            pltpu.VMEM((2, 32, KMAIN), BF16),
            pltpu.VMEM((3, LOADS, NSUB * 128), BF16),
            pltpu.VMEM((5, 10, LOADS, 128), F32),
            pltpu.VMEM((5, 10, LOADS, 128), F32),
            pltpu.VMEM((4, 2 * NROW, 8, 128), F32),
            pltpu.VMEM((4, NSUB // 2, 8, 128), F32),
            pltpu.VMEM((32, 128), F32),
            pltpu.VMEM((12, LOADS, 128), jnp.int32),
            pltpu.VMEM((8, 128), jnp.int32),
            pltpu.VMEM((32, WIDE), F32),
            pltpu.VMEM((32, WIDE), F32),
            pltpu.VMEM((32, WIDE), F32),
            pltpu.SemaphoreType.DMA((6,)),
            pltpu.SemaphoreType.DMA((FACES + 1,)),
            pltpu.SemaphoreType.DMA((FACES,)),
            pltpu.SemaphoreType.DMA((NSEM,)),
            pltpu.SemaphoreType.DMA((NSEM,)),
        ],
        compiler_params=pltpu.CompilerParams(
            collective_id=0, has_side_effects=True, vmem_limit_bytes=48 * 1024 * 1024
        ),
    )(forces, h, schur, coarse_inv, perm, corner_rows, corner_ids, corner_count)


def solution(mesh):
    in_specs = (
        P("sub", None, "row"),
        P("sub", "row", None),
        P("sub", "row", None),
        P(("sub", "row"), None),
        P("sub", None, "row"),
        P("sub", None),
        P("sub", None),
        P("sub"),
    )
    out_specs = (P("sub", None, "row"), P("sub", None, "row"))
    return jax.shard_map(body, mesh=mesh, in_specs=in_specs, out_specs=out_specs, check_vma=False)
```

```python
import functools

import jax
import jax.numpy as jnp
from jax import lax
from jax.experimental import pallas as pl
from jax.experimental.pallas import tpu as pltpu
from jax.sharding import PartitionSpec as P

MESH = pl.DeviceIdType.MESH
HIGHEST = lax.Precision.HIGHEST
F32 = jnp.float32
BF16 = jnp.bfloat16

NSUB = 32
NROW = 4
LOADS = 16
FACES = 6
FACEQ = 96
WIDE = FACES * 128
BLOCK = 650
NS = 2600
KMAIN = 2560
KFULL = 2688
PART = 640
SPILL = 768
SLOTS = 48

IDS, FORCES, TPART, CFULL, HCORN, XG, CORN, JUMP, ARA, ARB = 0, 1, 2, 3, 4, 5, 9, 12, 17, 21
XL = 25
NSEM = 29


def lanes(shape):
    return lax.broadcasted_iota(jnp.int32, shape, 1)


def dot_nt(a, b, precision=None):
    return lax.dot_general(
        a, b, (((1,), (1,)), ((), ())), precision=precision, preferred_element_type=F32
    )


def dot_nn(a, b, precision=None):
    return lax.dot_general(
        a, b, (((1,), (0,)), ((), ())), precision=precision, preferred_element_type=F32
    )


def dot_tn(a, b, precision=None):
    return lax.dot_general(
        a, b, (((0,), (0,)), ((), ())), precision=precision, preferred_element_type=F32
    )


def lane_gather(x, idx):
    dims = lax.GatherDimensionNumbers(
        offset_dims=(),
        collapsed_slice_dims=(1,),
        start_index_map=(1,),
        operand_batching_dims=(0,),
        start_indices_batching_dims=(0,),
    )
    return lax.gather(
        x, idx[..., None], dims, (1, 1), mode=lax.GatherScatterMode.PROMISE_IN_BOUNDS
    )


def pack_tiles(pieces, shift, count):
    rows = pieces[0].shape[0]
    lane = lanes((rows, 128))
    tiles = [jnp.zeros((rows, 128), F32) for _ in range(count)]
    for f, piece in enumerate(pieces):
        a, b0 = divmod(FACEQ * f, 128)
        b = shift + b0
        if isinstance(b, int) and b == 0:
            rolled = piece
        else:
            rolled = pltpu.roll(piece, b, 1)
        if b0 == 0:
            tiles[a] = tiles[a] + rolled
        else:
            tiles[a] = tiles[a] + jnp.where(lane >= b, rolled, 0.0)
            if a + 1 < count:
                tiles[a + 1] = tiles[a + 1] + jnp.where(lane < b, rolled, 0.0)
    return tiles


def eliminate(m):
    wide = (LOADS, 128)
    row_id = lax.broadcasted_iota(jnp.int32, wide, 0)
    cols = [jnp.broadcast_to(m[:, k : k + 1], wide) for k in range(LOADS)]
    for k in range(LOADS):
        scale = 1.0 / jnp.broadcast_to(cols[k][k : k + 1, :], wide)

        def step(x):
            row = jnp.broadcast_to(x[k : k + 1, :], wide) * scale
            return jnp.where(row_id == k, row, x - cols[k] * row)

        m = step(m)
        for j in range(k + 1, LOADS):
            cols[j] = step(cols[j])
    return pltpu.roll(m, 112, 1)


def kernel(
    forces_in, h_hbm, s_hbm, c_in, perm_in, rows_in, ids_in, count_in, mult_out, res_out,
    forces, c_own, perm, corner_rows, corner_ids, count,
    raw_h, raw_s, hv, sv, ht, ib, tb, ca, cat, kt, fb, ft, xf, oh, hco, hcb, hcf, xb, xl, xw, cb, sb, jb, ra, rb, gs, pidx,
    small, dv, rv, mv, in_sem, h_sem, s_sem, send, recv,
):
    g = lax.axis_index("sub")
    q = lax.axis_index("row")
    core = lax.rem(g, 2)
    zc = lax.rem(g // 2, 4)
    xc = g // 8

    def dev(x, z, c):
        return (x * 4 + z) * 2 + c

    def away(i):
        return (1 - i // 2) * (2 + i) + (i // 2) * (3 - i)

    def peer(k):
        x = lax.rem(xc + away(k // 8), 4)
        z = lax.rem(zc + away(lax.rem(k // 2, 4)), 4)
        return dev(x, z, lax.rem(core + 1 + lax.rem(k, 2), 2))

    def load(src, dst, sem, f):
        size = FACEQ if f < FACES else BLOCK - FACES * FACEQ
        rows = pl.ds(FACEQ * f, size)
        return pltpu.make_async_copy(src.at[rows], dst.at[rows], sem.at[f])

    inputs = [
        pltpu.make_async_copy(src, dst, in_sem.at[i])
        for i, (src, dst) in enumerate(
            [(ids_in, corner_ids), (count_in, count), (forces_in, forces), (rows_in, corner_rows)]
            + [(c_in, c_own), (perm_in, perm)]
        )
    ]
    for copy in inputs:
        copy.start()
    for f in range(FACES + 1):
        load(h_hbm, raw_h, h_sem, f).start()

    barrier = pltpu.get_barrier_semaphore()

    @pl.loop(0, NSUB - 1)
    def _(k):
        pl.semaphore_signal(barrier, inc=1, device_id=(peer(k), q), device_id_type=MESH)

    other = g + 1 - 2 * core
    for k in range(1, NROW):
        far = lax.rem(q + k, NROW)
        pl.semaphore_signal(barrier, inc=1, device_id=(g, far), device_id_type=MESH)
        pl.semaphore_signal(barrier, inc=1, device_id=(other, far), device_id_type=MESH)

    for f in range(FACES):
        load(s_hbm, raw_s, s_sem, f).start()

    for copy in inputs:
        copy.wait()
    lane8 = lanes((8, 128))

    def slot_row(ref, first, second):
        small[...] = jnp.full((8, 128), -1, jnp.int32)
        small[0:2, 0:24] = ref[...]
        top = jnp.broadcast_to(small[0:1, :], (8, 128))
        low = pltpu.roll(jnp.broadcast_to(small[1:2, :], (8, 128)), 24, 1)
        out = jnp.where(lane8 < first, top, -1)
        return jnp.where((lane8 >= 24) & (lane8 < 24 + second), low, out)

    live = slot_row(corner_ids, jnp.minimum(count[0], 24), jnp.minimum(count[1], 24))
    both = pltpu.roll(live, SLOTS, 1)
    ib[g] = jnp.where(lane8 < SLOTS, live, jnp.where(lane8 < 2 * SLOTS, both, -1))

    shift = 10 * q
    lane32 = lanes((32, 128))
    last = jnp.zeros((32, 128), F32)
    ft[...] = last
    for s in range(2):
        ft[LOADS * s : LOADS * s + LOADS, 0 : BLOCK - PART] = forces[s, :, PART:BLOCK]
    for t in range(6):
        if t < 5:
            now = jnp.concatenate([forces[s, :, 128 * t : 128 * t + 128] for s in range(2)], axis=0)
        else:
            now = ft[...]
        now = pltpu.roll(now, shift, 1)
        fb[q, :, 128 * t : 128 * t + 128] = jnp.where(lane32 >= shift, now, last).astype(BF16)
        last = now

    rows = slot_row(corner_rows, 24, 24).astype(F32)
    spot = jnp.broadcast_to(rows[0:1, :], (128, 128)).T[:SLOTS].astype(jnp.int32)
    lane24 = lanes((24, 128))
    lane48 = lanes((SLOTS, 128))
    rest = jnp.zeros((8, 128), F32)
    for t in range(KFULL // 128):
        for s in range(2):
            hit = jnp.where(lane24 + 128 * t == spot[24 * s : 24 * s + 24], 1.0, 0.0)
            oh[s, :, 128 * t : 128 * t + 128] = jnp.concatenate([hit, rest], axis=0).astype(BF16)
    for s in range(2):
        for f in range(FACES):
            hv[s, 128 * f + FACEQ : 128 * f + 128, :] = jnp.zeros((32, KFULL), BF16)
        hv[s, :, KMAIN:] = jnp.zeros((WIDE, KFULL - KMAIN), BF16)
        ht[s, :, KMAIN:] = jnp.zeros((128, KFULL - KMAIN), BF16)
    hco[...] = jnp.zeros((128, WIDE), BF16)

    def split(raw, start, dst, at, count):
        @pl.loop(0, count)
        def _(i):
            pair = jnp.swapaxes(raw[pl.ds(start + 16 * i, 16)], 0, 1)
            for s in range(2):
                dst[s, pl.ds(pl.multiple_of(at + 16 * i, 16), 16), :NS] = pair[s]

    for f in range(FACES):
        load(h_hbm, raw_h, h_sem, f).wait()
        split(raw_h, FACEQ * f, hv, 128 * f, FACEQ // 16)
    load(h_hbm, raw_h, h_sem, FACES).wait()
    split(raw_h, FACEQ * FACES, ht, 0, 5)

    pl.semaphore_wait(barrier, NSUB - 1 + 2 * (NROW - 1))

    def to_plane(src_of, dst, sem):
        @pl.loop(0, NSUB - 1)
        def _(k):
            far = peer(k)
            pltpu.make_async_remote_copy(
                src_ref=src_of(far),
                dst_ref=dst,
                send_sem=send.at[sem],
                recv_sem=recv.at[sem],
                device_id=(far, q),
                device_id_type=MESH,
            ).start()

    def to_row(ref, sem):
        for k in (2, 1, 3):
            pltpu.make_async_remote_copy(
                src_ref=ref,
                dst_ref=ref,
                send_sem=send.at[sem],
                recv_sem=recv.at[sem],
                device_id=(g, lax.rem(q + k, NROW)),
                device_id_type=MESH,
            ).start()

    drains = []

    def arrived(ref, sem):
        pltpu.make_async_copy(ref, ref, recv.at[sem]).wait()
        drains.append((ref, sem))

    to_plane(lambda far: ib.at[g], ib.at[g], IDS)
    to_row(fb.at[q], FORCES)

    corner_h = jnp.concatenate([dot_nt(oh[s], hv[s])[:24] for s in range(2)], axis=0)
    corner_t = jnp.concatenate([dot_nt(oh[s], ht[s])[:24] for s in range(2)], axis=0)
    corner_t = jnp.where(lane48 < BLOCK - FACES * FACEQ, corner_t, 0.0)
    hco[:SLOTS, :] = corner_h.astype(BF16)
    pieces = [corner_h[:, 128 * f : 128 * f + 128] for f in range(FACES)] + [corner_t]
    for t, tile in enumerate(pack_tiles(pieces, shift, 6)):
        hcb[q, :, 128 * t : 128 * t + 128] = tile.astype(BF16)

    to_row(hcb.at[q], HCORN)

    arrived(ib.at[pl.ds(0, NSUB - 1)], IDS)

    def pick_columns(far):
        idx = ib[far]
        tile = lax.shift_right_arithmetic(idx, 7)
        lane = lax.bitwise_and(idx, 127)
        total = jnp.zeros((8, 128), F32)
        for v in range(8):
            got = lane_gather(c_own[:, 128 * v : 128 * v + 128], lane)
            total = total + jnp.where(tile == v, got, 0.0)
        return total

    ca[g] = pick_columns(g)

    @pl.loop(0, NSUB - 1)
    def _(k):
        far = peer(k)
        tb[far] = pick_columns(far)
        pltpu.make_async_remote_copy(
            src_ref=tb.at[far],
            dst_ref=ca.at[g],
            send_sem=send.at[TPART],
            recv_sem=recv.at[TPART],
            device_id=(far, q),
            device_id_type=MESH,
        ).start()

    def assemble(slots, put):
        for p in range(NROW):
            first = slots[p, :, 0:128]
            if p > 0:
                first = first + slots[p - 1, :, PART:SPILL]
            put(PART * p, first)
            put(PART * p + 128, slots[p, :, 128:PART])
        put(KMAIN, slots[NROW - 1, :, PART:SPILL])

    arrived(fb.at[pl.ds(0, NROW - 1)], FORCES)

    def put_forces(start, value):
        xf[:, start : start + value.shape[1]] = value

    assemble(fb, put_forces)

    arrived(hcb.at[pl.ds(0, NROW - 1)], HCORN)
    hcf[96:128, :] = jnp.zeros((32, KFULL), BF16)

    def put_corner(start, value):
        width = value.shape[1]
        hcf[:SLOTS, start : start + width] = value
        hcf[SLOTS : 2 * SLOTS, start : start + width] = value

    assemble(hcb, put_corner)

    lane16 = lanes((LOADS, 128))
    first_sub = (lane16 < 24) | ((lane16 >= 48) & (lane16 < 72))
    own_cols = pl.ds(pl.multiple_of(128 * g, 128), 128)

    def corner_send(n, both):
        at = jnp.where(first_sub, both[:LOADS], both[LOADS:])
        high = at.astype(BF16).astype(F32)
        cb[n, :, own_cols] = jnp.where(lane16 < SLOTS, high, at - high).astype(BF16)
        to_plane(lambda far: cb.at[n, :, own_cols], cb.at[n, :, own_cols], CORN + n)

    corner_send(0, dot_nt(xf[...], hcf[...]))

    arrived(ca.at[pl.ds(0, NSUB - 1)], TPART)
    for half in range(2):
        block = ca[16 * half : 16 * half + 16].reshape(128, 128)
        cat[q, :, 128 * half : 128 * half + 128] = block.T[:SLOTS]
    to_row(cat.at[q], CFULL)

    for s in range(2):
        rv[LOADS * s : LOADS * s + LOADS, :] = dot_nt(xf[LOADS * s : LOADS * s + LOADS, :], hv[s])

    for f in range(FACES):
        for t in range(2):
            pidx[FACES * t + f] = jnp.full((LOADS, 128), 127, jnp.int32)
            pidx[FACES * t + f, :, :FACEQ] = jnp.broadcast_to(perm[f, t : t + 1, :], (LOADS, FACEQ))
    kt[96:128, :] = jnp.zeros((32, NSUB * 128), BF16)
    gs[...] = jnp.zeros((32, 128), F32)
    for s in range(2):
        for f in range(FACES):
            sv[s, 128 * f + FACEQ : 128 * f + 128, :] = jnp.zeros((32, NS), BF16)
    for f in range(FACES):
        load(s_hbm, raw_s, s_sem, f).wait()
        split(raw_s, FACEQ * f, sv, 128 * f, FACEQ // 16)

    arrived(cat.at[pl.ds(0, NROW - 1)], CFULL)

    slot_lane = lanes((SLOTS, 128))

    @pl.loop(0, NSUB // 2)
    def _(pair):
        c = jnp.where(lane8 < SLOTS, ib[2 * pair], ib[2 * pair + 1])
        tile = 2 * lax.bitwise_and(lax.shift_right_arithmetic(c, 3), 3) + lax.shift_right_arithmetic(c, 9)
        tile = jnp.where(c < 0, -1, tile)
        lane = 8 * lax.bitwise_and(lax.shift_right_arithmetic(c, 5), 15) + lax.bitwise_and(c, 7)
        parts = []
        for a in range(SLOTS // 8):
            total = jnp.zeros((8, 128), F32)
            for v in range(8):
                got = lane_gather(cat[v // 2, 8 * a : 8 * a + 8, 128 * (v % 2) : 128 * (v % 2) + 128], lane)
                total = total + jnp.where(tile == v, got, 0.0)
            parts.append(total)
        total = jnp.concatenate(parts, axis=0)
        first = jnp.where(slot_lane < SLOTS, total, pltpu.roll(total, SLOTS, 1))
        second = jnp.where(slot_lane < SLOTS, pltpu.roll(total, 128 - SLOTS, 1), total)
        for i, part in enumerate((first, second)):
            part = jnp.where(slot_lane < 2 * SLOTS, part, 0.0)
            high = part.astype(BF16)
            cols = pl.ds(pl.multiple_of(256 * pair + 128 * i, 128), 128)
            kt[:SLOTS, cols] = high
            kt[SLOTS : 2 * SLOTS, cols] = (part - high.astype(F32)).astype(BF16)

    def corner_finish(n, flex):
        arrived(cb.at[n, :, pl.ds(0, (NSUB - 1) * 128)], CORN + n)
        spread = dot_nt(cb[n], kt[...])
        spread = spread + pltpu.roll(spread, 128 - SLOTS, 1)
        left = jnp.concatenate(
            [
                jnp.where(lane16 < 24, spread, 0.0),
                jnp.where((lane16 >= 24) & (lane16 < SLOTS), spread, 0.0),
            ],
            axis=0,
        ).astype(BF16)
        return flex + dot_nn(left, hco[...])

    face_targets = {
        2: dev(xc, lax.rem(zc + 3, 4), core),
        3: dev(xc, lax.rem(zc + 1, 4), core),
        4: dev(lax.rem(xc + 3, 4), zc, core),
        5: dev(lax.rem(xc + 1, 4), zc, core),
    }

    def face_of(v, t, f):
        return v[LOADS * t : LOADS * t + LOADS, 128 * f : 128 * f + 128]

    def jump_send(n, v):
        sb[n, 0] = face_of(v, 0, 0)
        sb[n, 1] = face_of(v, 1, 1)
        for f in range(2, FACES):
            for t in range(2):
                sb[n, 2 * f - 2 + t] = face_of(v, t, f)
        moves = [(0, 1, 1, other), (1, 0, 1, other)]
        moves += [(2 * f - 2, 2 * (f ^ 1) - 2, 2, face_targets[f]) for f in range(2, FACES)]
        for src, dst, size, far in moves:
            pltpu.make_async_remote_copy(
                src_ref=sb.at[n, pl.ds(src, size)],
                dst_ref=jb.at[n, pl.ds(dst, size)],
                send_sem=send.at[JUMP + n],
                recv_sem=recv.at[JUMP + n],
                device_id=(far, q),
                device_id_type=MESH,
            ).start()

    def jump_finish(n, v):
        arrived(jb.at[n], JUMP + n)
        subs = []
        for t in range(2):
            out = []
            for f in range(FACES):
                if f < 2:
                    remote = jb[n, f] if f == t else face_of(v, 1 - t, f ^ 1)
                else:
                    remote = jb[n, 2 * f - 2 + t]
                out.append(face_of(v, t, f) - lane_gather(remote, pidx[FACES * t + f]))
            subs.append(jnp.concatenate(out, axis=1))
        return jnp.concatenate(subs, axis=0)

    own_part = pl.ds(pl.multiple_of(PART * q, 128), PART)

    def gather_send(n, x):
        pieces = [x[:, 128 * f : 128 * f + 128] for f in range(FACES)]
        whole = jnp.concatenate(pack_tiles(pieces, shift, 5), axis=1)
        high = whole.astype(BF16)
        xb[n, :, own_part] = high
        to_row(xb.at[n, :, own_part], XG + n)
        xl[n, :, own_part] = (whole - high.astype(F32)).astype(BF16)
        to_row(xl.at[n, :, own_part], XL + n)

    def gather_high(n):
        arrived(xb.at[n, :, pl.ds(0, 3 * PART)], XG + n)

    def gather_low(n):
        arrived(xl.at[n, :, pl.ds(0, 3 * PART)], XL + n)

    def full(n):
        return xb[n].astype(F32) + xl[n].astype(F32)

    def product(x, mat):
        return jnp.concatenate(
            [dot_nt(x[:LOADS, :], mat[0, :, :KMAIN]), dot_nt(x[LOADS:, :], mat[1, :, :KMAIN])],
            axis=0,
        )

    chip_pos = NROW * core + q
    chip_id = g // 2

    def inner_start(n, x, y):
        total = jnp.zeros((32, 32), F32)
        for s in range(2):
            xs, ys = x[LOADS * s : LOADS * s + LOADS], y[LOADS * s : LOADS * s + LOADS]
            total = total + dot_nt(
                jnp.concatenate([xs, ys], axis=0), jnp.concatenate([ys, xs], axis=0), HIGHEST
            )
        gs[:, :32] = total
        plain = jnp.where(lane16 < LOADS, gs[:LOADS], 0.0)
        turned = jnp.where(lane16 < LOADS, pltpu.roll(gs[LOADS:], 112, 1), 0.0)
        sym = plain + turned
        plain = plain + plain
        ra[n, chip_pos] = (
            plain[:8] + pltpu.roll(plain[8:], 16, 1) + pltpu.roll(sym[:8], 32, 1) + pltpu.roll(sym[8:], 48, 1)
        )
        for k in (2, 6, 1, 3, 5, 7, 4):
            pos = lax.rem(chip_pos + k, 2 * NROW)
            pltpu.make_async_remote_copy(
                src_ref=ra.at[n, chip_pos],
                dst_ref=ra.at[n, chip_pos],
                send_sem=send.at[ARA + n],
                recv_sem=recv.at[ARA + n],
                device_id=(2 * chip_id + pos // NROW, lax.rem(pos, NROW)),
                device_id_type=MESH,
            ).start()

    def tree(values):
        while len(values) > 1:
            values = [a + b for a, b in zip(values[::2], values[1::2])]
        return values[0]

    def inner_middle(n):
        arrived(ra.at[n, pl.ds(0, 2 * NROW - 1)], ARA + n)
        rb[n, chip_id] = tree([ra[n, i] for i in range(2 * NROW)])

        @pl.loop(0, NSUB // 2 - 1)
        def _(k):
            far = lax.rem(xc + away(k // 4), 4) * 4 + lax.rem(zc + away(lax.rem(k, 4)), 4)
            pltpu.make_async_remote_copy(
                src_ref=rb.at[n, chip_id],
                dst_ref=rb.at[n, chip_id],
                send_sem=send.at[ARB + n],
                recv_sem=recv.at[ARB + n],
                device_id=(2 * far + core, q),
                device_id_type=MESH,
            ).start()

    def inner_finish(n):
        arrived(rb.at[n, pl.ds(0, NSUB // 2 - 1)], ARB + n)
        total = tree([rb[n, i] for i in range(NSUB // 2)])
        plain = jnp.concatenate([total, pltpu.roll(total, 112, 1)], axis=0)
        sym = jnp.concatenate([pltpu.roll(total, 96, 1), pltpu.roll(total, 80, 1)], axis=0)
        return plain, sym

    def solve(a, b):
        return eliminate(
            jnp.where(lane16 < LOADS, a, jnp.where(lane16 < 2 * LOADS, pltpu.roll(b, 16, 1), 0.0))
        )

    def combine(x, coeffs):
        small = coeffs[:, :LOADS]
        return jnp.concatenate(
            [dot_tn(small, x[:LOADS], HIGHEST), dot_tn(small, x[LOADS:], HIGHEST)], axis=0
        )

    v = corner_finish(0, rv[...])
    jump_send(0, v)
    rv[...] = jump_finish(0, v)

    gather_send(0, rv[...])
    gather_high(0)
    y = product(xb.at[0], sv)
    jump_send(1, y)
    inner_start(0, rv[...], y)
    dv[...] = jump_finish(1, y)

    gather_send(1, dv[...])
    gather_low(0)
    gather_high(1)
    corner_send(1, dot_nt(xb[1], hcf[:, :KMAIN]))
    inner_middle(0)
    flex = product(xb.at[1], hv)
    v = corner_finish(1, flex)
    jump_send(2, v)
    inner_start(1, dv[...], v)
    gather_low(1)
    energy, energy_sym = inner_finish(0)
    row16 = lax.broadcasted_iota(jnp.int32, (LOADS, 128), 0)
    energy_inv = solve(energy_sym, jnp.where(row16 == lane16, 1.0, 0.0))
    image = jump_finish(2, v)
    gather_send(2, image)
    inner_middle(1)
    unused, curvature = inner_finish(1)
    step = solve(curvature, energy)
    rv[...] = rv[...] - combine(image, step)
    gather_high(2)
    gather_low(2)
    xw[0] = (full(0) - combine(full(2), step)).astype(BF16)
    y = product(xw.at[0], sv)
    jump_send(3, y)
    inner_start(2, rv[...], y)
    mv[...] = combine(dv[...], step)
    zvec = jump_finish(3, y)
    gather_send(3, zvec)
    inner_middle(2)
    energy_next, unused = inner_finish(2)
    blend = dot_nn(energy_inv[:, :LOADS], energy_next[:, :LOADS], HIGHEST)
    dv[...] = zvec + combine(dv[...], blend)

    gather_high(3)
    gather_low(3)
    xw[1] = (full(3) + combine(full(1), blend)).astype(BF16)
    corner_send(2, dot_nt(xw[1], hcf[:, :KMAIN]))
    flex = product(xw.at[1], hv)
    v = corner_finish(2, flex)
    inner_start(3, dv[...], v)
    jump_send(4, v)
    inner_middle(3)
    image = jump_finish(4, v)
    unused, curvature = inner_finish(3)
    step = solve(curvature, energy_next)

    def put_out(ref, value):
        tiles = pack_tiles([value[:, 128 * f : 128 * f + 128] for f in range(FACES)], 0, 5)
        for s in range(2):
            for t in range(5):
                ref[s, :, 128 * t : 128 * t + 128] = tiles[t][LOADS * s : LOADS * s + LOADS]
            ref[s, :, PART:BLOCK] = jnp.zeros((LOADS, BLOCK - PART), F32)

    put_out(mult_out, mv[...] + combine(dv[...], step))
    put_out(res_out, rv[...] - combine(image, step))

    for ref, sem in drains:
        pltpu.make_async_copy(ref, ref, send.at[sem]).wait()


def body(
    forces, inverse_h, schur_matrix, coarse_inv, face_perm, corner_rows, corner_ids, corner_count
):
    h = jnp.transpose(inverse_h, (1, 0, 2))
    schur = jnp.transpose(schur_matrix, (1, 0, 2))
    perm = jnp.transpose(face_perm, (1, 0, 2))
    vmem = pl.BlockSpec(memory_space=pltpu.VMEM)
    hbm = pl.BlockSpec(memory_space=pltpu.MemorySpace.HBM)
    out = jax.ShapeDtypeStruct((2, LOADS, BLOCK), F32)
    return pl.pallas_call(
        kernel,
        out_shape=(out, out),
        in_specs=[hbm] * 8,
        out_specs=(vmem, vmem),
        scratch_shapes=[
            pltpu.VMEM((2, LOADS, BLOCK), F32),
            pltpu.VMEM((8, 1024), F32),
            pltpu.VMEM((FACES, 2, FACEQ), jnp.int32),
            pltpu.VMEM((2, 24), jnp.int32),
            pltpu.VMEM((2, 24), jnp.int32),
            pltpu.SMEM((2,), jnp.int32),
            pltpu.VMEM((656, 2, NS), BF16),
            pltpu.VMEM((FACES * FACEQ, 2, NS), BF16),
            pltpu.VMEM((2, WIDE, KFULL), BF16),
            pltpu.VMEM((2, WIDE, NS), BF16),
            pltpu.VMEM((2, 128, KFULL), BF16),
            pltpu.VMEM((NSUB, 8, 128), jnp.int32),
            pltpu.VMEM((NSUB, 8, 128), F32),
            pltpu.VMEM((NSUB, 8, 128), F32),
            pltpu.VMEM((NROW, SLOTS, 256), F32),
            pltpu.VMEM((128, NSUB * 128), BF16),
            pltpu.VMEM((NROW, 32, SPILL), BF16),
            pltpu.VMEM((32, 128), F32),
            pltpu.VMEM((32, KFULL), BF16),
            pltpu.VMEM((2, 32, KFULL), BF16),
            pltpu.VMEM((128, WIDE), BF16),
            pltpu.VMEM((NROW, SLOTS, SPILL), BF16),
            pltpu.VMEM((128, KFULL), BF16),
            pltpu.VMEM((4, 32, KMAIN), BF16),
            pltpu.VMEM((4, 32, KMAIN), BF16),
            pltpu.VMEM((2, 32, KMAIN), BF16),
            pltpu.VMEM((3, LOADS, NSUB * 128), BF16),
            pltpu.VMEM((5, 10, LOADS, 128), F32),
            pltpu.VMEM((5, 10, LOADS, 128), F32),
            pltpu.VMEM((4, 2 * NROW, 8, 128), F32),
            pltpu.VMEM((4, NSUB // 2, 8, 128), F32),
            pltpu.VMEM((32, 128), F32),
            pltpu.VMEM((12, LOADS, 128), jnp.int32),
            pltpu.VMEM((8, 128), jnp.int32),
            pltpu.VMEM((32, WIDE), F32),
            pltpu.VMEM((32, WIDE), F32),
            pltpu.VMEM((32, WIDE), F32),
            pltpu.SemaphoreType.DMA((6,)),
            pltpu.SemaphoreType.DMA((FACES + 1,)),
            pltpu.SemaphoreType.DMA((FACES,)),
            pltpu.SemaphoreType.DMA((NSEM,)),
            pltpu.SemaphoreType.DMA((NSEM,)),
        ],
        compiler_params=pltpu.CompilerParams(
            collective_id=0, has_side_effects=True, vmem_limit_bytes=65000 * 1024
        ),
    )(forces, h, schur, coarse_inv, perm, corner_rows, corner_ids, corner_count)


def solution(mesh):
    in_specs = (
        P("sub", None, "row"),
        P("sub", "row", None),
        P("sub", "row", None),
        P(("sub", "row"), None),
        P("sub", None, "row"),
        P("sub", None),
        P("sub", None),
        P("sub"),
    )
    out_specs = (P("sub", None, "row"), P("sub", None, "row"))
    return jax.shard_map(body, mesh=mesh, in_specs=in_specs, out_specs=out_specs, check_vma=False)
```

```python
import functools

import jax
import jax.numpy as jnp
from jax import lax
from jax.experimental import pallas as pl
from jax.experimental.pallas import tpu as pltpu
from jax.sharding import PartitionSpec as P

MESH = pl.DeviceIdType.MESH
HIGHEST = lax.Precision.HIGHEST
F32 = jnp.float32
BF16 = jnp.bfloat16

NSUB = 32
NROW = 4
LOADS = 16
FACES = 6
FACEQ = 96
WIDE = FACES * 128
BLOCK = 650
NS = 2600
KMAIN = 2560
KFULL = 2688
PART = 640
SPILL = 768
SLOTS = 48

IDS, FORCES, TPART, CFULL, HCORN, XG, CORN, JUMP, ARA, ARB = 0, 1, 2, 3, 4, 5, 9, 12, 17, 21
XL = 25
NSEM = 29


def lanes(shape):
    return lax.broadcasted_iota(jnp.int32, shape, 1)


def dot_nt(a, b, precision=None):
    return lax.dot_general(
        a, b, (((1,), (1,)), ((), ())), precision=precision, preferred_element_type=F32
    )


def dot_nn(a, b, precision=None):
    return lax.dot_general(
        a, b, (((1,), (0,)), ((), ())), precision=precision, preferred_element_type=F32
    )


def dot_tn(a, b, precision=None):
    return lax.dot_general(
        a, b, (((0,), (0,)), ((), ())), precision=precision, preferred_element_type=F32
    )


def lane_gather(x, idx):
    dims = lax.GatherDimensionNumbers(
        offset_dims=(),
        collapsed_slice_dims=(1,),
        start_index_map=(1,),
        operand_batching_dims=(0,),
        start_indices_batching_dims=(0,),
    )
    return lax.gather(
        x, idx[..., None], dims, (1, 1), mode=lax.GatherScatterMode.PROMISE_IN_BOUNDS
    )


def pack_tiles(pieces, shift, count):
    rows = pieces[0].shape[0]
    lane = lanes((rows, 128))
    tiles = [jnp.zeros((rows, 128), F32) for _ in range(count)]
    for f, piece in enumerate(pieces):
        a, b0 = divmod(FACEQ * f, 128)
        b = shift + b0
        if isinstance(b, int) and b == 0:
            rolled = piece
        else:
            rolled = pltpu.roll(piece, b, 1)
        if b0 == 0:
            tiles[a] = tiles[a] + rolled
        else:
            tiles[a] = tiles[a] + jnp.where(lane >= b, rolled, 0.0)
            if a + 1 < count:
                tiles[a + 1] = tiles[a + 1] + jnp.where(lane < b, rolled, 0.0)
    return tiles


def eliminate(m):
    wide = (LOADS, 128)
    row_id = lax.broadcasted_iota(jnp.int32, wide, 0)
    cols = [jnp.broadcast_to(m[:, k : k + 1], wide) for k in range(LOADS)]
    for k in range(LOADS):
        scale = 1.0 / jnp.broadcast_to(cols[k][k : k + 1, :], wide)

        def step(x):
            row = jnp.broadcast_to(x[k : k + 1, :], wide) * scale
            return jnp.where(row_id == k, row, x - cols[k] * row)

        m = step(m)
        for j in range(k + 1, LOADS):
            cols[j] = step(cols[j])
    return pltpu.roll(m, 112, 1)


def kernel(
    forces_in, h_hbm, s_hbm, c_in, perm_in, rows_in, ids_in, count_in, mult_out, res_out,
    forces, c_own, perm, corner_rows, corner_ids, count,
    raw_h, raw_s, hv, sv, ht, ib, tb, ca, cat, kt, fb, ft, xf, oh, hco, hcb, hcf, xb, xl, xw, cb, sb, jb, ra, rb, gs, pidx,
    small, dv, rv, mv, in_sem, h_sem, s_sem, send, recv,
):
    g = lax.axis_index("sub")
    q = lax.axis_index("row")
    core = lax.rem(g, 2)
    zc = lax.rem(g // 2, 4)
    xc = g // 8

    def dev(x, z, c):
        return (x * 4 + z) * 2 + c

    def away(i):
        return (1 - i // 2) * (2 + i) + (i // 2) * (3 - i)

    def peer(k):
        x = lax.rem(xc + away(k // 8), 4)
        z = lax.rem(zc + away(lax.rem(k // 2, 4)), 4)
        return dev(x, z, lax.rem(core + 1 + lax.rem(k, 2), 2))

    def load(src, dst, sem, f):
        size = FACEQ if f < FACES else BLOCK - FACES * FACEQ
        rows = pl.ds(FACEQ * f, size)
        return pltpu.make_async_copy(src.at[rows], dst.at[rows], sem.at[f])

    inputs = [
        pltpu.make_async_copy(src, dst, in_sem.at[i])
        for i, (src, dst) in enumerate(
            [(ids_in, corner_ids), (count_in, count), (forces_in, forces), (rows_in, corner_rows)]
            + [(c_in, c_own), (perm_in, perm)]
        )
    ]
    for copy in inputs:
        copy.start()
    for f in range(FACES + 1):
        load(h_hbm, raw_h, h_sem, f).start()

    barrier = pltpu.get_barrier_semaphore()

    @pl.loop(0, NSUB - 1)
    def _(k):
        pl.semaphore_signal(barrier, inc=1, device_id=(peer(k), q), device_id_type=MESH)

    other = g + 1 - 2 * core
    for k in range(1, NROW):
        far = lax.rem(q + k, NROW)
        pl.semaphore_signal(barrier, inc=1, device_id=(g, far), device_id_type=MESH)
        pl.semaphore_signal(barrier, inc=1, device_id=(other, far), device_id_type=MESH)

    for f in range(FACES):
        load(s_hbm, raw_s, s_sem, f).start()

    for copy in inputs:
        copy.wait()
    lane8 = lanes((8, 128))

    def slot_row(ref, first, second):
        small[...] = jnp.full((8, 128), -1, jnp.int32)
        small[0:2, 0:24] = ref[...]
        top = jnp.broadcast_to(small[0:1, :], (8, 128))
        low = pltpu.roll(jnp.broadcast_to(small[1:2, :], (8, 128)), 24, 1)
        out = jnp.where(lane8 < first, top, -1)
        return jnp.where((lane8 >= 24) & (lane8 < 24 + second), low, out)

    live = slot_row(corner_ids, jnp.minimum(count[0], 24), jnp.minimum(count[1], 24))
    both = pltpu.roll(live, SLOTS, 1)
    ib[g] = jnp.where(lane8 < SLOTS, live, jnp.where(lane8 < 2 * SLOTS, both, -1))

    shift = 10 * q
    lane32 = lanes((32, 128))
    last = jnp.zeros((32, 128), F32)
    ft[...] = last
    for s in range(2):
        ft[LOADS * s : LOADS * s + LOADS, 0 : BLOCK - PART] = forces[s, :, PART:BLOCK]
    for t in range(6):
        if t < 5:
            now = jnp.concatenate([forces[s, :, 128 * t : 128 * t + 128] for s in range(2)], axis=0)
        else:
            now = ft[...]
        now = pltpu.roll(now, shift, 1)
        fb[q, :, 128 * t : 128 * t + 128] = jnp.where(lane32 >= shift, now, last).astype(BF16)
        last = now

    rows = slot_row(corner_rows, 24, 24).astype(F32)
    spot = jnp.broadcast_to(rows[0:1, :], (128, 128)).T[:SLOTS].astype(jnp.int32)
    lane24 = lanes((24, 128))
    lane48 = lanes((SLOTS, 128))
    rest = jnp.zeros((8, 128), F32)
    for t in range(KFULL // 128):
        for s in range(2):
            hit = jnp.where(lane24 + 128 * t == spot[24 * s : 24 * s + 24], 1.0, 0.0)
            oh[s, :, 128 * t : 128 * t + 128] = jnp.concatenate([hit, rest], axis=0).astype(BF16)
    for s in range(2):
        for f in range(FACES):
            hv[s, 128 * f + FACEQ : 128 * f + 128, :] = jnp.zeros((32, KFULL), BF16)
        hv[s, :, KMAIN:] = jnp.zeros((WIDE, KFULL - KMAIN), BF16)
        ht[s, :, KMAIN:] = jnp.zeros((128, KFULL - KMAIN), BF16)
    hco[...] = jnp.zeros((128, WIDE), BF16)

    def split(raw, start, dst, at, count):
        @pl.loop(0, count)
        def _(i):
            pair = jnp.swapaxes(raw[pl.ds(start + 16 * i, 16)], 0, 1)
            for s in range(2):
                dst[s, pl.ds(pl.multiple_of(at + 16 * i, 16), 16), :NS] = pair[s]

    for f in range(FACES):
        load(h_hbm, raw_h, h_sem, f).wait()
        split(raw_h, FACEQ * f, hv, 128 * f, FACEQ // 16)
    load(h_hbm, raw_h, h_sem, FACES).wait()
    split(raw_h, FACEQ * FACES, ht, 0, 5)

    pl.semaphore_wait(barrier, NSUB - 1 + 2 * (NROW - 1))

    def to_plane(src_of, dst, sem):
        @pl.loop(0, NSUB - 1)
        def _(k):
            far = peer(k)
            pltpu.make_async_remote_copy(
                src_ref=src_of(far),
                dst_ref=dst,
                send_sem=send.at[sem],
                recv_sem=recv.at[sem],
                device_id=(far, q),
                device_id_type=MESH,
            ).start()

    def to_row(ref, sem):
        for k in (2, 1, 3):
            pltpu.make_async_remote_copy(
                src_ref=ref,
                dst_ref=ref,
                send_sem=send.at[sem],
                recv_sem=recv.at[sem],
                device_id=(g, lax.rem(q + k, NROW)),
                device_id_type=MESH,
            ).start()

    drains = []

    def drain():
        while drains:
            ref, sem = drains.pop()
            pltpu.make_async_copy(ref, ref, send.at[sem]).wait()

    def arrived(ref, sem):
        pltpu.make_async_copy(ref, ref, recv.at[sem]).wait()
        drains.append((ref, sem))

    to_plane(lambda far: ib.at[g], ib.at[g], IDS)
    to_row(fb.at[q], FORCES)

    corner_h = jnp.concatenate([dot_nt(oh[s], hv[s])[:24] for s in range(2)], axis=0)
    corner_t = jnp.concatenate([dot_nt(oh[s], ht[s])[:24] for s in range(2)], axis=0)
    corner_t = jnp.where(lane48 < BLOCK - FACES * FACEQ, corner_t, 0.0)
    hco[:SLOTS, :] = corner_h.astype(BF16)
    pieces = [corner_h[:, 128 * f : 128 * f + 128] for f in range(FACES)] + [corner_t]
    for t, tile in enumerate(pack_tiles(pieces, shift, 6)):
        hcb[q, :, 128 * t : 128 * t + 128] = tile.astype(BF16)

    to_row(hcb.at[q], HCORN)

    arrived(ib.at[pl.ds(0, NSUB - 1)], IDS)

    def pick_columns(far):
        idx = ib[far]
        tile = lax.shift_right_arithmetic(idx, 7)
        lane = lax.bitwise_and(idx, 127)
        total = jnp.zeros((8, 128), F32)
        for v in range(8):
            got = lane_gather(c_own[:, 128 * v : 128 * v + 128], lane)
            total = total + jnp.where(tile == v, got, 0.0)
        return total

    ca[g] = pick_columns(g)

    @pl.loop(0, NSUB - 1)
    def _(k):
        far = peer(k)
        tb[far] = pick_columns(far)
        pltpu.make_async_remote_copy(
            src_ref=tb.at[far],
            dst_ref=ca.at[g],
            send_sem=send.at[TPART],
            recv_sem=recv.at[TPART],
            device_id=(far, q),
            device_id_type=MESH,
        ).start()

    def assemble(slots, put):
        for p in range(NROW):
            first = slots[p, :, 0:128]
            if p > 0:
                first = first + slots[p - 1, :, PART:SPILL]
            put(PART * p, first)
            put(PART * p + 128, slots[p, :, 128:PART])
        put(KMAIN, slots[NROW - 1, :, PART:SPILL])

    arrived(fb.at[pl.ds(0, NROW - 1)], FORCES)

    def put_forces(start, value):
        xf[:, start : start + value.shape[1]] = value

    assemble(fb, put_forces)

    arrived(hcb.at[pl.ds(0, NROW - 1)], HCORN)
    hcf[96:128, :] = jnp.zeros((32, KFULL), BF16)

    def put_corner(start, value):
        width = value.shape[1]
        hcf[:SLOTS, start : start + width] = value
        hcf[SLOTS : 2 * SLOTS, start : start + width] = value

    assemble(hcb, put_corner)

    lane16 = lanes((LOADS, 128))
    first_sub = (lane16 < 24) | ((lane16 >= 48) & (lane16 < 72))
    own_cols = pl.ds(pl.multiple_of(128 * g, 128), 128)

    def corner_send(n, both):
        at = jnp.where(first_sub, both[:LOADS], both[LOADS:])
        high = at.astype(BF16).astype(F32)
        cb[n, :, own_cols] = jnp.where(lane16 < SLOTS, high, at - high).astype(BF16)
        to_plane(lambda far: cb.at[n, :, own_cols], cb.at[n, :, own_cols], CORN + n)

    corner_send(0, dot_nt(xf[...], hcf[...]))

    arrived(ca.at[pl.ds(0, NSUB - 1)], TPART)
    for half in range(2):
        block = ca[16 * half : 16 * half + 16].reshape(128, 128)
        cat[q, :, 128 * half : 128 * half + 128] = block.T[:SLOTS]
    to_row(cat.at[q], CFULL)

    for s in range(2):
        rv[LOADS * s : LOADS * s + LOADS, :] = dot_nt(xf[LOADS * s : LOADS * s + LOADS, :], hv[s])

    for f in range(FACES):
        for t in range(2):
            pidx[FACES * t + f] = jnp.full((LOADS, 128), 127, jnp.int32)
            pidx[FACES * t + f, :, :FACEQ] = jnp.broadcast_to(perm[f, t : t + 1, :], (LOADS, FACEQ))
    kt[96:128, :] = jnp.zeros((32, NSUB * 128), BF16)
    gs[...] = jnp.zeros((32, 128), F32)
    for s in range(2):
        for f in range(FACES):
            sv[s, 128 * f + FACEQ : 128 * f + 128, :] = jnp.zeros((32, NS), BF16)
    for f in range(FACES):
        load(s_hbm, raw_s, s_sem, f).wait()
        split(raw_s, FACEQ * f, sv, 128 * f, FACEQ // 16)

    arrived(cat.at[pl.ds(0, NROW - 1)], CFULL)

    slot_lane = lanes((SLOTS, 128))

    @pl.loop(0, NSUB // 2)
    def _(pair):
        c = jnp.where(lane8 < SLOTS, ib[2 * pair], ib[2 * pair + 1])
        tile = 2 * lax.bitwise_and(lax.shift_right_arithmetic(c, 3), 3) + lax.shift_right_arithmetic(c, 9)
        tile = jnp.where(c < 0, -1, tile)
        lane = 8 * lax.bitwise_and(lax.shift_right_arithmetic(c, 5), 15) + lax.bitwise_and(c, 7)
        parts = []
        for a in range(SLOTS // 8):
            total = jnp.zeros((8, 128), F32)
            for v in range(8):
                got = lane_gather(cat[v // 2, 8 * a : 8 * a + 8, 128 * (v % 2) : 128 * (v % 2) + 128], lane)
                total = total + jnp.where(tile == v, got, 0.0)
            parts.append(total)
        total = jnp.concatenate(parts, axis=0)
        first = jnp.where(slot_lane < SLOTS, total, pltpu.roll(total, SLOTS, 1))
        second = jnp.where(slot_lane < SLOTS, pltpu.roll(total, 128 - SLOTS, 1), total)
        for i, part in enumerate((first, second)):
            part = jnp.where(slot_lane < 2 * SLOTS, part, 0.0)
            high = part.astype(BF16)
            cols = pl.ds(pl.multiple_of(256 * pair + 128 * i, 128), 128)
            kt[:SLOTS, cols] = high
            kt[SLOTS : 2 * SLOTS, cols] = (part - high.astype(F32)).astype(BF16)

    def corner_finish(n, flex):
        arrived(cb.at[n, :, pl.ds(0, (NSUB - 1) * 128)], CORN + n)
        spread = dot_nt(cb[n], kt[...])
        spread = spread + pltpu.roll(spread, 128 - SLOTS, 1)
        left = jnp.concatenate(
            [
                jnp.where(lane16 < 24, spread, 0.0),
                jnp.where((lane16 >= 24) & (lane16 < SLOTS), spread, 0.0),
            ],
            axis=0,
        ).astype(BF16)
        return flex + dot_nn(left, hco[...])

    face_targets = {
        2: dev(xc, lax.rem(zc + 3, 4), core),
        3: dev(xc, lax.rem(zc + 1, 4), core),
        4: dev(lax.rem(xc + 3, 4), zc, core),
        5: dev(lax.rem(xc + 1, 4), zc, core),
    }

    def face_of(v, t, f):
        return v[LOADS * t : LOADS * t + LOADS, 128 * f : 128 * f + 128]

    def jump_send(n, v):
        sb[n, 0] = face_of(v, 0, 0)
        sb[n, 1] = face_of(v, 1, 1)
        for f in range(2, FACES):
            for t in range(2):
                sb[n, 2 * f - 2 + t] = face_of(v, t, f)
        moves = [(0, 1, 1, other), (1, 0, 1, other)]
        moves += [(2 * f - 2, 2 * (f ^ 1) - 2, 2, face_targets[f]) for f in range(2, FACES)]
        for src, dst, size, far in moves:
            pltpu.make_async_remote_copy(
                src_ref=sb.at[n, pl.ds(src, size)],
                dst_ref=jb.at[n, pl.ds(dst, size)],
                send_sem=send.at[JUMP + n],
                recv_sem=recv.at[JUMP + n],
                device_id=(far, q),
                device_id_type=MESH,
            ).start()

    def jump_finish(n, v):
        arrived(jb.at[n], JUMP + n)
        subs = []
        for t in range(2):
            out = []
            for f in range(FACES):
                if f < 2:
                    remote = jb[n, f] if f == t else face_of(v, 1 - t, f ^ 1)
                else:
                    remote = jb[n, 2 * f - 2 + t]
                out.append(face_of(v, t, f) - lane_gather(remote, pidx[FACES * t + f]))
            subs.append(jnp.concatenate(out, axis=1))
        return jnp.concatenate(subs, axis=0)

    own_part = pl.ds(pl.multiple_of(PART * q, 128), PART)

    def gather_send(n, x):
        pieces = [x[:, 128 * f : 128 * f + 128] for f in range(FACES)]
        whole = jnp.concatenate(pack_tiles(pieces, shift, 5), axis=1)
        high = whole.astype(BF16)
        xb[n, :, own_part] = high
        to_row(xb.at[n, :, own_part], XG + n)
        xl[n, :, own_part] = (whole - high.astype(F32)).astype(BF16)
        to_row(xl.at[n, :, own_part], XL + n)

    def gather_high(n):
        arrived(xb.at[n, :, pl.ds(0, 3 * PART)], XG + n)

    def gather_low(n):
        arrived(xl.at[n, :, pl.ds(0, 3 * PART)], XL + n)

    def full(n):
        return xb[n].astype(F32) + xl[n].astype(F32)

    def product(x, mat):
        return jnp.concatenate(
            [dot_nt(x[:LOADS, :], mat[0, :, :KMAIN]), dot_nt(x[LOADS:, :], mat[1, :, :KMAIN])],
            axis=0,
        )

    chip_pos = NROW * core + q
    chip_id = g // 2

    def inner_start(n, x, y):
        total = jnp.zeros((32, 32), F32)
        for s in range(2):
            xs, ys = x[LOADS * s : LOADS * s + LOADS], y[LOADS * s : LOADS * s + LOADS]
            total = total + dot_nt(
                jnp.concatenate([xs, ys], axis=0), jnp.concatenate([ys, xs], axis=0), HIGHEST
            )
        gs[:, :32] = total
        plain = jnp.where(lane16 < LOADS, gs[:LOADS], 0.0)
        turned = jnp.where(lane16 < LOADS, pltpu.roll(gs[LOADS:], 112, 1), 0.0)
        sym = plain + turned
        plain = plain + plain
        ra[n, chip_pos] = (
            plain[:8] + pltpu.roll(plain[8:], 16, 1) + pltpu.roll(sym[:8], 32, 1) + pltpu.roll(sym[8:], 48, 1)
        )
        for k in (2, 6, 1, 3, 5, 7, 4):
            pos = lax.rem(chip_pos + k, 2 * NROW)
            pltpu.make_async_remote_copy(
                src_ref=ra.at[n, chip_pos],
                dst_ref=ra.at[n, chip_pos],
                send_sem=send.at[ARA + n],
                recv_sem=recv.at[ARA + n],
                device_id=(2 * chip_id + pos // NROW, lax.rem(pos, NROW)),
                device_id_type=MESH,
            ).start()

    def tree(values):
        while len(values) > 1:
            values = [a + b for a, b in zip(values[::2], values[1::2])]
        return values[0]

    def inner_middle(n):
        arrived(ra.at[n, pl.ds(0, 2 * NROW - 1)], ARA + n)
        rb[n, chip_id] = tree([ra[n, i] for i in range(2 * NROW)])

        @pl.loop(0, NSUB // 2 - 1)
        def _(k):
            far = lax.rem(xc + away(k // 4), 4) * 4 + lax.rem(zc + away(lax.rem(k, 4)), 4)
            pltpu.make_async_remote_copy(
                src_ref=rb.at[n, chip_id],
                dst_ref=rb.at[n, chip_id],
                send_sem=send.at[ARB + n],
                recv_sem=recv.at[ARB + n],
                device_id=(2 * far + core, q),
                device_id_type=MESH,
            ).start()

    def inner_finish(n):
        arrived(rb.at[n, pl.ds(0, NSUB // 2 - 1)], ARB + n)
        total = tree([rb[n, i] for i in range(NSUB // 2)])
        plain = jnp.concatenate([total, pltpu.roll(total, 112, 1)], axis=0)
        sym = jnp.concatenate([pltpu.roll(total, 96, 1), pltpu.roll(total, 80, 1)], axis=0)
        return plain, sym

    def solve(a, b):
        return eliminate(
            jnp.where(lane16 < LOADS, a, jnp.where(lane16 < 2 * LOADS, pltpu.roll(b, 16, 1), 0.0))
        )

    def combine(x, coeffs):
        small = coeffs[:, :LOADS]
        return jnp.concatenate(
            [dot_tn(small, x[:LOADS], HIGHEST), dot_tn(small, x[LOADS:], HIGHEST)], axis=0
        )

    v = corner_finish(0, rv[...])
    jump_send(0, v)
    rv[...] = jump_finish(0, v)

    gather_send(0, rv[...])
    gather_high(0)
    y = product(xb.at[0], sv)
    jump_send(1, y)
    inner_start(0, rv[...], y)
    dv[...] = jump_finish(1, y)

    gather_send(1, dv[...])
    gather_low(0)
    gather_high(1)
    corner_send(1, dot_nt(xb[1], hcf[:, :KMAIN]))
    inner_middle(0)
    flex = product(xb.at[1], hv)
    v = corner_finish(1, flex)
    jump_send(2, v)
    inner_start(1, dv[...], v)
    gather_low(1)
    energy, energy_sym = inner_finish(0)
    row16 = lax.broadcasted_iota(jnp.int32, (LOADS, 128), 0)
    energy_inv = solve(energy_sym, jnp.where(row16 == lane16, 1.0, 0.0))
    image = jump_finish(2, v)
    gather_send(2, image)
    inner_middle(1)
    unused, curvature = inner_finish(1)
    step = solve(curvature, energy)
    rv[...] = rv[...] - combine(image, step)
    gather_high(2)
    gather_low(2)
    xw[0] = (full(0) - combine(full(2), step)).astype(BF16)
    y = product(xw.at[0], sv)
    jump_send(3, y)
    inner_start(2, rv[...], y)
    mv[...] = combine(dv[...], step)
    zvec = jump_finish(3, y)
    gather_send(3, zvec)
    inner_middle(2)
    energy_next, unused = inner_finish(2)
    blend = dot_nn(energy_inv[:, :LOADS], energy_next[:, :LOADS], HIGHEST)
    dv[...] = zvec + combine(dv[...], blend)

    gather_high(3)
    gather_low(3)
    xw[1] = (full(3) + combine(full(1), blend)).astype(BF16)
    corner_send(2, dot_nt(xw[1], hcf[:, :KMAIN]))
    flex = product(xw.at[1], hv)
    v = corner_finish(2, flex)
    inner_start(3, dv[...], v)
    jump_send(4, v)
    drain()
    inner_middle(3)
    image = jump_finish(4, v)
    unused, curvature = inner_finish(3)
    step = solve(curvature, energy_next)

    def put_out(ref, value):
        tiles = pack_tiles([value[:, 128 * f : 128 * f + 128] for f in range(FACES)], 0, 5)
        for s in range(2):
            for t in range(5):
                ref[s, :, 128 * t : 128 * t + 128] = tiles[t][LOADS * s : LOADS * s + LOADS]
            ref[s, :, PART:BLOCK] = jnp.zeros((LOADS, BLOCK - PART), F32)

    put_out(mult_out, mv[...] + combine(dv[...], step))
    put_out(res_out, rv[...] - combine(image, step))

    drain()


def body(
    forces, inverse_h, schur_matrix, coarse_inv, face_perm, corner_rows, corner_ids, corner_count
):
    h = jnp.transpose(inverse_h, (1, 0, 2))
    schur = jnp.transpose(schur_matrix, (1, 0, 2))
    perm = jnp.transpose(face_perm, (1, 0, 2))
    vmem = pl.BlockSpec(memory_space=pltpu.VMEM)
    hbm = pl.BlockSpec(memory_space=pltpu.MemorySpace.HBM)
    out = jax.ShapeDtypeStruct((2, LOADS, BLOCK), F32)
    return pl.pallas_call(
        kernel,
        out_shape=(out, out),
        in_specs=[hbm] * 8,
        out_specs=(vmem, vmem),
        scratch_shapes=[
            pltpu.VMEM((2, LOADS, BLOCK), F32),
            pltpu.VMEM((8, 1024), F32),
            pltpu.VMEM((FACES, 2, FACEQ), jnp.int32),
            pltpu.VMEM((2, 24), jnp.int32),
            pltpu.VMEM((2, 24), jnp.int32),
            pltpu.SMEM((2,), jnp.int32),
            pltpu.VMEM((656, 2, NS), BF16),
            pltpu.VMEM((FACES * FACEQ, 2, NS), BF16),
            pltpu.VMEM((2, WIDE, KFULL), BF16),
            pltpu.VMEM((2, WIDE, NS), BF16),
            pltpu.VMEM((2, 128, KFULL), BF16),
            pltpu.VMEM((NSUB, 8, 128), jnp.int32),
            pltpu.VMEM((NSUB, 8, 128), F32),
            pltpu.VMEM((NSUB, 8, 128), F32),
            pltpu.VMEM((NROW, SLOTS, 256), F32),
            pltpu.VMEM((128, NSUB * 128), BF16),
            pltpu.VMEM((NROW, 32, SPILL), BF16),
            pltpu.VMEM((32, 128), F32),
            pltpu.VMEM((32, KFULL), BF16),
            pltpu.VMEM((2, 32, KFULL), BF16),
            pltpu.VMEM((128, WIDE), BF16),
            pltpu.VMEM((NROW, SLOTS, SPILL), BF16),
            pltpu.VMEM((128, KFULL), BF16),
            pltpu.VMEM((4, 32, KMAIN), BF16),
            pltpu.VMEM((4, 32, KMAIN), BF16),
            pltpu.VMEM((2, 32, KMAIN), BF16),
            pltpu.VMEM((3, LOADS, NSUB * 128), BF16),
            pltpu.VMEM((5, 10, LOADS, 128), F32),
            pltpu.VMEM((5, 10, LOADS, 128), F32),
            pltpu.VMEM((4, 2 * NROW, 8, 128), F32),
            pltpu.VMEM((4, NSUB // 2, 8, 128), F32),
            pltpu.VMEM((32, 128), F32),
            pltpu.VMEM((12, LOADS, 128), jnp.int32),
            pltpu.VMEM((8, 128), jnp.int32),
            pltpu.VMEM((32, WIDE), F32),
            pltpu.VMEM((32, WIDE), F32),
            pltpu.VMEM((32, WIDE), F32),
            pltpu.SemaphoreType.DMA((6,)),
            pltpu.SemaphoreType.DMA((FACES + 1,)),
            pltpu.SemaphoreType.DMA((FACES,)),
            pltpu.SemaphoreType.DMA((NSEM,)),
            pltpu.SemaphoreType.DMA((NSEM,)),
        ],
        compiler_params=pltpu.CompilerParams(
            collective_id=0, has_side_effects=True, vmem_limit_bytes=65000 * 1024
        ),
    )(forces, h, schur, coarse_inv, perm, corner_rows, corner_ids, corner_count)


def solution(mesh):
    in_specs = (
        P("sub", None, "row"),
        P("sub", "row", None),
        P("sub", "row", None),
        P(("sub", "row"), None),
        P("sub", None, "row"),
        P("sub", None),
        P("sub", None),
        P("sub"),
    )
    out_specs = (P("sub", None, "row"), P("sub", None, "row"))
    return jax.shard_map(body, mesh=mesh, in_specs=in_specs, out_specs=out_specs, check_vma=False)
```
